32 devices in a mesh: groups: 2 (over y), chan: 4 (over z), img: 4 (over x, core).
Axes of the slice: x: 2, y: 2, z: 4, core: 2. Of those that a mesh axis runs over, the one named last changes fastest.
Arguments:
- features: bfloat16 [8, 16, 16, 2048], P(('groups', 'img'), None, None, 'chan'), parts along dimension 0, may hold values from -6 to 6
- kernel_one: bfloat16 [3, 3, 2048, 2048], P(None, None, 'img', 'chan'), may hold values from -0.046875 to 0.046875
- kernel_two: bfloat16 [3, 3, 2048, 2048], P(None, None, 'img', 'chan'), may hold values from -0.046875 to 0.046875
Outputs:
- second_out: bfloat16 [8, 16, 16, 2048], P(('groups', 'img'), None, None, 'chan'), parts along dimension 0
The draws below stay inside these ranges and needn't reach their ends.
There are 2 independent parts, one for each index of `groups`. The reference program is written for one: setup_inputs(seed, part) draws one part's arguments, and reference() takes and returns one part's arrays. A program takes and returns all parts, laid end to end along the dimension named above; an argument that names none is the same for every part. Nothing has to cross between parts.
All inputs are finite; a program needn't handle non-finite values.
Results may differ from the reference program's by a relative error of at most 0.005.
Values may be sent and summed in bfloat16 or wider, within the bound.
No kernel may reach another device: no remote copies, remote signals or barrier semaphores. Data moves between devices by JAX's collectives and lax.ppermute only.
A program may use at most 64 MiB of HBM per device.

```python
import jax
import jax.numpy as jnp

C = 2048
IMG_H = 16
IMG_W = 16
FRAMES = 4


def steps_of(stream_key, shape, split, low, high):
    def one(axis_at, parts):
        draws = jax.random.uniform(jax.random.fold_in(jax.random.fold_in(stream_key, 6), axis_at), (parts,), jnp.float32, low / len(split), high / len(split))
        return jnp.repeat(jnp.exp(draws), shape[axis_at] // parts).reshape((-1,) + (1,) * (len(shape) - axis_at - 1))

    level = one(*split[0])
    for cut in split[1:]:
        level = level * one(*cut)
    return level


def bell_draw(own_key, dims, scale, limit, cuts=(), held_as=jnp.bfloat16):
    values = scale * jax.random.normal(own_key, dims, jnp.float32)
    if cuts:
        values = values * steps_of(own_key, dims, cuts, -0.22, 0.18)
    return jnp.clip(values, -limit, limit).astype(held_as)


def setup_inputs(seed: int = 0, part: int = 0) -> dict:
    keys = jax.random.split(jax.random.key(seed), 4)
    part_splits = jax.random.split(jax.random.fold_in(keys[3], part), 4)
    features = bell_draw(part_splits[0], (FRAMES, IMG_H, IMG_W, C), 1.0, 6.0, ((0, 4), (3, 4)))
    kernel_one = bell_draw(keys[1], (3, 3, C, C), (9 * C) ** -0.5, 0.046875, ((2, 4), (3, 4)))
    kernel_two = bell_draw(keys[2], (3, 3, C, C), (9 * C) ** -0.5, 0.046875, ((2, 4), (3, 4)))
    return {"features": features, "kernel_one": kernel_one, "kernel_two": kernel_two}


def pad_frames(active):
    return jnp.pad(active, ((0, 0), (1, 1), (1, 1), (0, 0)))


def conv_padded(padded, kernel):
    frame_count = padded.shape[0]
    height = padded.shape[1] - 2
    breadth = padded.shape[2] - 2
    summed = jnp.zeros((frame_count * height * breadth, kernel.shape[3]), jnp.float32)
    for offset_y in range(3):
        for offset_x in range(3):
            window = padded[:, offset_y:offset_y + height, offset_x:offset_x + breadth, :]
            window = window.reshape(frame_count * height * breadth, padded.shape[3])
            summed = summed + jnp.dot(window, kernel[offset_y, offset_x], preferred_element_type=jnp.float32)
    return summed.reshape(frame_count, height, breadth, kernel.shape[3])


def reference(features, kernel_one, kernel_two):
    first = conv_padded(pad_frames(features), kernel_one)
    hidden = jax.nn.silu(first).astype(jnp.bfloat16)
    return conv_padded(pad_frames(hidden), kernel_two).astype(jnp.bfloat16)
```

```python
import functools

import jax
import jax.numpy as jnp
from jax import lax
from jax.experimental import pallas as pl
from jax.experimental.pallas import tpu as pltpu
from jax.sharding import PartitionSpec as P

VMEM = pl.BlockSpec(memory_space=pltpu.VMEM)
F32, BF16 = jnp.float32, jnp.bfloat16


class Plan:
    def __init__(self, mesh, features, kernel):
        self.levels = mesh.shape["chan"]
        self.cols = mesh.shape["img"]
        self.ratio = self.levels // self.cols
        self.height, self.width = features.shape[1], features.shape[2]
        self.pixels = self.height * self.width
        self.piece = features.shape[3]
        self.c_in, self.c_out = kernel.shape[2], kernel.shape[3]
        self.share = self.pixels // self.cols
        self.bits = self.cols.bit_length() - 1

    def spread_pairs(self, d, e):
        pairs = []
        for k in range(self.levels):
            for f in range(self.cols):
                level = (f - d) % self.cols * self.ratio + (k % self.ratio - e) % self.ratio
                pairs.append((k * self.cols + f, level * self.cols + k // self.ratio))
        return pairs

    def swap(self, x, bit):
        return lax.ppermute(x, "img", [(i, i ^ (1 << bit)) for i in range(self.cols)])

    def spread(self, x):
        return [
            lax.ppermute(x, ("chan", "img"), self.spread_pairs(d, e))
            for d in range(self.cols)
            for e in range(self.ratio)
        ]

    def call(self, body, inputs, outputs, scratch=(), flops=0):
        moved = sum(x.size * x.dtype.itemsize for x in inputs)
        return pl.pallas_call(
            body,
            in_specs=[VMEM] * len(inputs),
            out_specs=[VMEM] * len(outputs),
            out_shape=[jax.ShapeDtypeStruct(*o) for o in outputs],
            scratch_shapes=list(scratch),
            cost_estimate=pl.CostEstimate(flops=flops, bytes_accessed=moved, transcendentals=0),
            compiler_params=pltpu.CompilerParams(vmem_limit_bytes=24 * 2**20),
        )(*inputs)


def place(plan, rows, frame, row_at, lane_at, wide):
    x = rows.astype(F32)
    column = lax.broadcasted_iota(jnp.int32, x.shape, 0) % plan.width
    left = jnp.where(column == 0, 0.0, pltpu.roll(x, 1, 0))
    right = jnp.where(column == plan.width - 1, 0.0, pltpu.roll(x, x.shape[0] - 1, 0))
    for b, moved in enumerate((left, x, right)):
        lanes = b * plan.c_in + lane_at
        if not isinstance(lanes, int):
            lanes = pl.multiple_of(lanes, 128)
        wide[frame, pl.ds(row_at, x.shape[0]), pl.ds(lanes, plan.piece)] = moved.astype(BF16)


def clear_edges(plan, frames, wide):
    zero = jnp.zeros((plan.width, wide.shape[2]), BF16)
    for f in range(frames):
        wide[f, 0 : plan.width, :] = zero
        wide[f, plan.width + plan.pixels :, :] = zero


def where_am_i(plan):
    level, col = lax.axis_index("chan"), lax.axis_index("img")
    return level // plan.ratio, level % plan.ratio, col


def first_row(plan, col):
    at, size = 0, plan.pixels
    for bit in range(plan.bits):
        size //= 2
        at = at + (col // 2**bit) % 2 * size
    return at


def conv_one_body(plan, frames, *refs):
    pieces = refs[: frames * plan.ratio]
    kernel, keep, send, wide = refs[frames * plan.ratio :]
    turn, lane, col = where_am_i(plan)
    clear_edges(plan, frames, wide)
    for f in range(frames):
        for e in range(plan.ratio):
            lane_at = (lane + e) % plan.ratio * plan.piece if plan.ratio > 1 else 0
            place(plan, pieces[f * plan.ratio + e][0], f, plan.width, lane_at, wide)
    half = plan.pixels // 2
    mine = col % 2 * half
    starts = (mine, half - mine)
    summed = None
    for a in range(3):
        parts = []
        for start in starts:
            rows = pl.ds(pl.multiple_of(start + a * plan.width, 16), half)
            parts.append(wide[:, rows, :].reshape(frames * half, 3 * plan.c_in))
        term = jnp.dot(
            jnp.concatenate(parts, axis=0),
            kernel[a].reshape(3 * plan.c_in, plan.c_out),
            preferred_element_type=F32,
        )
        summed = term if summed is None else summed + term
    keep[...] = summed[: frames * half].reshape(keep.shape)
    send[...] = summed[frames * half :].astype(BF16).reshape(send.shape)


def conv_one(plan, pieces, kernel):
    frames = len(pieces) // plan.ratio
    half = (frames, plan.pixels // 2, plan.c_out)
    return plan.call(
        functools.partial(conv_one_body, plan, frames),
        [*pieces, kernel],
        [(half, F32), (half, BF16)],
        [pltpu.VMEM((frames, plan.pixels + 2 * plan.width, 3 * plan.c_in), BF16)],
        18 * frames * plan.pixels * plan.c_in * plan.c_out,
    )


def halve_body(plan, bit, kept, came, keep, send):
    half = keep.shape[1]
    col = lax.axis_index("img")
    mine = (col // 2**bit) % 2 * half
    a = pl.ds(pl.multiple_of(mine, 16), half)
    b = pl.ds(pl.multiple_of(half - mine, 16), half)
    send[...] = (kept[:, b, :] + came[:, b, :].astype(F32)).astype(BF16)
    keep[...] = kept[:, a, :] + came[:, a, :].astype(F32)


def silu_body(kept, came, hidden):
    v = kept[...] + came[...].astype(F32)
    hidden[...] = (v / (1.0 + jnp.exp(-v))).astype(BF16)


def sum_one(plan, keep, send):
    for bit in range(1, plan.bits):
        came = plan.swap(send, bit - 1)
        half = (keep.shape[0], keep.shape[1] // 2, keep.shape[2])
        keep, send = plan.call(
            functools.partial(halve_body, plan, bit), [keep, came], [(half, F32), (half, BF16)]
        )
    came = plan.swap(send, plan.bits - 1)
    return plan.call(silu_body, [keep, came], [(keep.shape, BF16)])[0]


def conv_two_body(plan, frames, *refs):
    count = plan.cols * plan.ratio
    pieces = refs[:count]
    kernel, keep, send, wide = refs[count:]
    turn, lane, col = where_am_i(plan)
    clear_edges(plan, frames, wide)
    for d in range(plan.cols):
        row_at = pl.multiple_of(plan.width + first_row(plan, (turn + d) % plan.cols), 16)
        for e in range(plan.ratio):
            lane_at = (lane + e) % plan.ratio * plan.piece if plan.ratio > 1 else 0
            for f in range(frames):
                place(plan, pieces[d * plan.ratio + e][f], f, row_at, lane_at, wide)
    summed = None
    for a in range(3):
        rows = wide[:, a * plan.width : a * plan.width + plan.pixels, :]
        term = jnp.dot(
            rows.reshape(frames * plan.pixels, 3 * plan.c_in),
            kernel[a].reshape(3 * plan.c_in, plan.c_out),
            preferred_element_type=F32,
        )
        summed = term if summed is None else summed + term
    for f in range(frames):
        part = summed[f * plan.pixels : (f + 1) * plan.pixels]
        if f % 2 == 0:
            keep[f // 2] = part
        else:
            send[f // 2] = part.astype(BF16)


def conv_two(plan, pieces, kernel):
    frames = pieces[0].shape[0]
    half = (frames // 2, plan.pixels, plan.c_out)
    return plan.call(
        functools.partial(conv_two_body, plan, frames),
        [*pieces, kernel],
        [(half, F32), (half, BF16)],
        [pltpu.VMEM((frames, plan.pixels + 2 * plan.width, 3 * plan.c_in), BF16)],
        18 * frames * plan.pixels * plan.c_in * plan.c_out,
    )


def merge_body(plan, bit, count, *refs):
    kept, came = refs[:count], refs[count : 2 * count]
    outs = refs[2 * count :]
    kept = [(r, t) for r in kept for t in range(r.shape[0])]
    came = [(r, t) for r in came for t in range(r.shape[0])]
    col = lax.axis_index("img")
    low = (col // 2**bit) % 2 == 0
    for n, (ref, t) in enumerate(kept):
        before, behind = came[n - 1], came[n]
        got = jnp.where(low, before[0][before[1]].astype(F32), behind[0][behind[1]].astype(F32))
        total = ref[t] + got
        out = outs[n % 2]
        out[n // 2] = total.astype(out.dtype)


def sum_two(plan, parts):
    keeps, sends = [k for k, _ in parts], [s for _, s in parts]
    for bit in range(plan.bits):
        cames = [plan.swap(s, bit) for s in sends]
        count = sum(k.shape[0] for k in keeps)
        if count == 1:
            return plan.call(
                functools.partial(merge_body, plan, bit, 1),
                [*keeps, *cames],
                [((1, plan.pixels, plan.c_out), BF16)],
            )[0]
        half = (count // 2, plan.pixels, plan.c_out)
        keep, send = plan.call(
            functools.partial(merge_body, plan, bit, len(keeps)),
            [*keeps, *cames],
            [(half, F32), (half, BF16)],
        )
        keeps, sends = [keep], [send]


def shards(mesh, batches, features, kernel_one, kernel_two):
    plan = Plan(mesh, features, kernel_one)
    block = features.reshape(1, plan.pixels, plan.piece)
    pieces = plan.spread(block)
    size = plan.cols // batches
    parts = []
    for n in range(batches):
        own = pieces[n * size * plan.ratio : (n + 1) * size * plan.ratio]
        keep, send = conv_one(plan, own, kernel_one)
        hidden = sum_one(plan, keep, send)
        parts.append(conv_two(plan, plan.spread(hidden), kernel_two))
    return sum_two(plan, parts).reshape(features.shape)


def solution(mesh):
    placed = (
        P(("groups", "img"), None, None, "chan"),
        P(None, None, "img", "chan"),
        P(None, None, "img", "chan"),
    )
    return jax.shard_map(
        functools.partial(shards, mesh, 2),
        mesh=mesh,
        in_specs=placed,
        out_specs=P(("groups", "img"), None, None, "chan"),
        check_vma=False,
    )
```

```python
import functools

import jax
import jax.numpy as jnp
from jax import lax
from jax.experimental import pallas as pl
from jax.experimental.pallas import tpu as pltpu
from jax.sharding import PartitionSpec as P

VMEM = pl.BlockSpec(memory_space=pltpu.VMEM)
F32, BF16 = jnp.float32, jnp.bfloat16


def where_am_i():
    return lax.axis_index("chan"), lax.axis_index("img")


def after(x, *first):
    return lax.optimization_barrier((x, first))[0]


class Plan:
    def __init__(self, mesh, features, kernel):
        self.levels, self.cols = mesh.shape["chan"], mesh.shape["img"]
        self.pairs, self.ratio = self.cols // 2, self.levels // self.cols
        self.width = features.shape[2]
        self.pixels = features.shape[1] * features.shape[2]
        self.piece = features.shape[3]
        self.c_in, self.c_out = kernel.shape[2], kernel.shape[3]
        self.share = self.pixels // self.cols
        self.bits = self.cols.bit_length() - 1

    def wide(self, frames):
        return (frames, self.pixels + 2 * self.width, 3 * self.c_in)

    def spread_frame(self, x, turn):
        taken = []
        for e in range(self.ratio):
            moves = []
            for k in range(self.levels):
                for f in range(self.cols):
                    level = (f - turn) % self.cols * self.ratio + (k % self.ratio - e) % self.ratio
                    moves.append((k * self.cols + f, level * self.cols + k // self.ratio))
            taken.append(lax.ppermute(x, ("chan", "img"), moves))
        return taken

    def spread(self, x, turn):
        taken = []
        for e in range(self.ratio):
            moves = []
            for level in range(self.levels):
                v, u = level // self.ratio, level % self.ratio
                core, pair = v // self.pairs, (v + turn) % self.pairs
                for col in range(self.cols):
                    source = col * self.ratio + (u + e) % self.ratio
                    moves.append((source * self.cols + 2 * pair + core, level * self.cols + col))
            taken.append(lax.ppermute(x, ("chan", "img"), moves))
        return taken

    def lanes(self, level, e):
        if self.ratio == 1:
            return 0
        return pl.multiple_of((level + e) % self.ratio * self.piece, 128)

    def first_row(self, col):
        at, size = 0, self.pixels
        for bit in range(self.bits):
            size //= 2
            at = at + (col // 2**bit) % 2 * size
        return at

    def swap(self, x, bit):
        return lax.ppermute(x, "img", [(i, i ^ (1 << bit)) for i in range(self.cols)])

    def call(self, body, inputs, outputs, flops=0, scratch=()):
        moved = sum(x.size * x.dtype.itemsize for x in inputs)
        return pl.pallas_call(
            body,
            in_specs=[VMEM] * len(inputs),
            out_specs=[VMEM] * len(outputs),
            out_shape=[jax.ShapeDtypeStruct(*o) for o in outputs],
            scratch_shapes=list(scratch),
            cost_estimate=pl.CostEstimate(flops=flops, bytes_accessed=moved, transcendentals=0),
            compiler_params=pltpu.CompilerParams(vmem_limit_bytes=24 * 2**20),
        )(*inputs)


def stage_body(source, target, arrived):
    copy = pltpu.make_async_copy(source, target, arrived)
    copy.start()
    copy.wait()


def stage(kernel):
    return pl.pallas_call(
        stage_body,
        in_specs=[pl.BlockSpec(memory_space=pl.ANY)],
        out_specs=VMEM,
        out_shape=jax.ShapeDtypeStruct(kernel.shape, kernel.dtype),
        scratch_shapes=[pltpu.SemaphoreType.DMA],
        cost_estimate=pl.CostEstimate(flops=0, bytes_accessed=4 * kernel.size, transcendentals=0),
        compiler_params=pltpu.CompilerParams(vmem_limit_bytes=24 * 2**20),
    )(kernel)


def join_body(own, came, out):
    core = lax.axis_index("img") % 2
    out[pl.ds(core, 1)] = own[...].reshape((1,) + own.shape)
    out[pl.ds(1 - core, 1)] = came[...].reshape((1,) + came.shape)


def join(plan, own):
    return plan.call(join_body, [own, plan.swap(own, 0)], [((2,) + own.shape, own.dtype)])[0]


def place(plan, rows, frame, row_at, lane_at, wide):
    x = rows.astype(F32)
    column = lax.broadcasted_iota(jnp.int32, x.shape, 0) % plan.width
    left = jnp.where(column == 0, 0.0, pltpu.roll(x, 1, 0))
    right = jnp.where(column == plan.width - 1, 0.0, pltpu.roll(x, x.shape[0] - 1, 0))
    for b, moved in enumerate((left, x, right)):
        wide[frame, pl.ds(row_at, x.shape[0]), pl.ds(b * plan.c_in + lane_at, plan.piece)] = moved.astype(BF16)


def clear_edges(plan, wide):
    zero = jnp.zeros((plan.width, wide.shape[2]), BF16)
    for f in range(wide.shape[0]):
        wide[f, 0 : plan.width, :] = zero
        wide[f, plan.width + plan.pixels :, :] = zero


def times(plan, rows, kernel):
    summed = None
    for a in range(3):
        term = jnp.dot(rows(a), kernel[a].reshape(3 * plan.c_in, plan.c_out), preferred_element_type=F32)
        summed = term if summed is None else summed + term
    return summed


def half_rows(plan, wide, core, a):
    half = plan.pixels // 2
    rows = pl.ds(pl.multiple_of(core * half + a * plan.width, 16), half)
    return wide[:, rows, :].reshape(-1, 3 * plan.c_in)


def one_body(plan, *refs):
    pieces, (kernel, send, keep, wide) = refs[:-4], refs[-4:]
    level, col = where_am_i()
    clear_edges(plan, wide)
    for n, piece in enumerate(pieces):
        place(plan, piece[...], n // plan.ratio, plan.width, plan.lanes(level, n % plan.ratio), wide)
    halves = lambda a: jnp.concatenate([half_rows(plan, wide, core, a) for core in (1 - col % 2, col % 2)], axis=0)
    summed = times(plan, halves, kernel)
    size = summed.shape[0] // 2
    send[...] = summed[:size].astype(BF16).reshape(send.shape)
    keep[...] = summed[size:].reshape(keep.shape)


def conv_one(plan, pieces, kernel):
    frames = len(pieces) // plan.ratio
    half = (frames, plan.pixels // 2, plan.c_out)
    flops = 18 * frames * plan.pixels * plan.c_in * plan.c_out
    outputs = [(half, BF16), (half, F32)]
    scratch = [pltpu.VMEM(plan.wide(frames), BF16)]
    return plan.call(functools.partial(one_body, plan), [*pieces, kernel], outputs, flops, scratch)


def halve_body(bit, kept, came, keep, send):
    half = keep.shape[1]
    mine = (lax.axis_index("img") // 2**bit) % 2 * half
    a = pl.ds(pl.multiple_of(mine, 16), half)
    b = pl.ds(pl.multiple_of(half - mine, 16), half)
    send[...] = (kept[:, b, :] + came[:, b, :].astype(F32)).astype(BF16)
    keep[...] = kept[:, a, :] + came[:, a, :].astype(F32)


def silu_body(kept, came, hidden):
    v = kept[...] + came[...].astype(F32)
    hidden[...] = (v / (1.0 + jnp.exp(-v))).astype(BF16)


def halve(plan, bit, keep, came):
    half = (keep.shape[0], keep.shape[1] // 2, plan.c_out)
    return plan.call(functools.partial(halve_body, bit), [keep, came], [(half, F32), (half, BF16)])


def sum_one(plan, keep, came):
    keep, send = halve(plan, 1, keep, came)
    for bit in range(2, plan.bits):
        keep, send = halve(plan, bit, keep, plan.swap(send, bit - 1))
    return keep, send


def add_silu(plan, keep, came):
    return plan.call(silu_body, [keep, came], [(keep.shape, BF16)])[0]


def conv_two_body(plan, chosen, *refs):
    pieces, (kernel, out, wide) = refs[:-3], refs[-3:]
    level = lax.axis_index("chan")
    clear_edges(plan, wide)
    for n, piece in enumerate(pieces):
        turn, e = n // plan.ratio, n % plan.ratio
        pair = (level // plan.ratio + turn) % plan.pairs
        for core in range(2):
            row_at = pl.multiple_of(plan.width + plan.first_row(2 * pair + core), 16)
            for f, at in enumerate(chosen):
                place(plan, piece[core, at], f, row_at, plan.lanes(level, e), wide)
    rows = lambda a: wide[:, a * plan.width : a * plan.width + plan.pixels, :].reshape(-1, 3 * plan.c_in)
    out[...] = times(plan, rows, kernel).astype(out.dtype).reshape(out.shape)


def conv_two(plan, pieces, chosen, kernel, dtype):
    frames = len(chosen)
    return plan.call(
        functools.partial(conv_two_body, plan, chosen),
        [*pieces, kernel],
        [((frames, plan.pixels, plan.c_out), dtype)],
        18 * frames * plan.pixels * plan.c_in * plan.c_out,
        [pltpu.VMEM(plan.wide(frames), BF16)],
    )[0]


def aligned(bit, came, n):
    low = (lax.axis_index("img") // 2**bit) % 2 == 0
    return jnp.where(low, came[n - 1 if n else came.shape[0] - 1].astype(F32), came[n].astype(F32))


def merge_body(bit, at, kept, came, out):
    for n, t in enumerate(at):
        out[n] = (kept[n].astype(F32) + aligned(bit, came, t)).astype(out.dtype)


def merge(plan, bit, kept, came, at, dtype):
    body = functools.partial(merge_body, bit, at)
    return plan.call(body, [kept, came], [(kept.shape, dtype)])[0]


def last_body(kept, first, came, out):
    out[...] = (kept[...] + aligned(0, first, 0)[None] + came[...].astype(F32)).astype(BF16)


def sum_rest(plan, here, first, send):
    if plan.bits == 2:
        came = plan.swap(send, 1)
        return plan.call(last_body, [here, first, came], [(here.shape, BF16)])[0]
    keep = merge(plan, 0, here, first, range(0, 2 * here.shape[0], 2), F32)
    for bit in range(1, plan.bits):
        came = plan.swap(send, bit)
        count = keep.shape[0]
        total = merge(plan, bit, keep, came, range(count), F32 if count > 1 else BF16)
        keep, send = total[0::2], total[1::2].astype(BF16)
    return total


def shards(mesh, features, kernel_one, kernel_two):
    plan = Plan(mesh, features, kernel_one)
    block = features.reshape(plan.pixels, plan.piece)
    odd = list(range(1, plan.cols, 2))
    even = list(range(2, plan.cols, 4)) + list(range(0, plan.cols, 4))
    early = [p for d in odd for p in plan.spread_frame(block, d)]
    kernel_one = stage(kernel_one)
    late = [p for d in even for p in plan.spread_frame(block, d)]
    last = plan.bits - 1
    send, keep = conv_one(plan, early, kernel_one)
    keep, ahead = sum_one(plan, keep, after(plan.swap(send, 0), late))
    send, kept = conv_one(plan, after(late, ahead), kernel_one)
    hidden = join(plan, add_silu(plan, keep, after(plan.swap(ahead, last), send)))
    odds = [p for t in range(plan.pairs) for p in plan.spread(hidden, t)]
    keep, behind = sum_one(plan, kept, plan.swap(send, 0))
    hidden = join(plan, add_silu(plan, keep, plan.swap(behind, last)))
    evens = [p for t in range(plan.pairs) for p in plan.spread(hidden, t)]
    count = len(odd)
    sums = conv_two(plan, after(odds, hidden), range(count), kernel_two, BF16)
    came = plan.swap(after(sums, evens), 0)
    here = conv_two(plan, evens, range(count // 2), kernel_two, F32)
    send = merge(plan, 0, here, came, range(1, count, 2), BF16)
    here = conv_two(plan, evens, range(count // 2, count), kernel_two, F32)
    return sum_rest(plan, here, came, send).reshape(features.shape)


def solution(mesh):
    placed = (
        P(("groups", "img"), None, None, "chan"),
        P(None, None, "img", "chan"),
        P(None, None, "img", "chan"),
    )
    return jax.shard_map(
        functools.partial(shards, mesh),
        mesh=mesh,
        in_specs=placed,
        out_specs=P(("groups", "img"), None, None, "chan"),
        check_vma=False,
    )
```

```python
import functools

import jax
import jax.numpy as jnp
from jax import lax
from jax.experimental import pallas as pl
from jax.experimental.pallas import tpu as pltpu
from jax.sharding import PartitionSpec as P

VMEM = pl.BlockSpec(memory_space=pltpu.VMEM)
F32, BF16 = jnp.float32, jnp.bfloat16


def where_am_i():
    return lax.axis_index("chan"), lax.axis_index("img")


def after(x, *first):
    return lax.optimization_barrier((x, first))[0]


class Plan:
    def __init__(self, mesh, features, kernel):
        self.levels, self.cols = mesh.shape["chan"], mesh.shape["img"]
        self.pairs, self.ratio = self.cols // 2, self.levels // self.cols
        self.width = features.shape[2]
        self.pixels = features.shape[1] * features.shape[2]
        self.piece = features.shape[3]
        self.c_in, self.c_out = kernel.shape[2], kernel.shape[3]
        self.share = self.pixels // self.cols
        self.bits = self.cols.bit_length() - 1

    def wide(self, frames):
        return (frames, self.pixels + 2 * self.width, 3 * self.c_in)

    def spread_frame(self, x, turn):
        taken = []
        for e in range(self.ratio):
            moves = []
            for k in range(self.levels):
                for f in range(self.cols):
                    level = (f - turn) % self.cols * self.ratio + (k % self.ratio - e) % self.ratio
                    moves.append((k * self.cols + f, level * self.cols + k // self.ratio))
            taken.append(lax.ppermute(x, ("chan", "img"), moves))
        return taken

    def spread(self, x, turn):
        taken = []
        for e in range(self.ratio):
            moves = []
            for level in range(self.levels):
                v, u = level // self.ratio, level % self.ratio
                core, pair = v // self.pairs, (v + turn) % self.pairs
                for col in range(self.cols):
                    source = col * self.ratio + (u + e) % self.ratio
                    moves.append((source * self.cols + 2 * pair + core, level * self.cols + col))
            taken.append(lax.ppermute(x, ("chan", "img"), moves))
        return taken

    def lanes(self, level, e):
        if self.ratio == 1:
            return 0
        return pl.multiple_of((level + e) % self.ratio * self.piece, 128)

    def first_row(self, col):
        at, size = 0, self.pixels
        for bit in range(self.bits):
            size //= 2
            at = at + (col // 2**bit) % 2 * size
        return at

    def swap(self, x, bit):
        return lax.ppermute(x, "img", [(i, i ^ (1 << bit)) for i in range(self.cols)])

    def call(self, body, inputs, outputs, flops=0, scratch=()):
        moved = sum(x.size * x.dtype.itemsize for x in inputs)
        return pl.pallas_call(
            body,
            in_specs=[VMEM] * len(inputs),
            out_specs=[VMEM] * len(outputs),
            out_shape=[jax.ShapeDtypeStruct(*o) for o in outputs],
            scratch_shapes=list(scratch),
            cost_estimate=pl.CostEstimate(flops=flops, bytes_accessed=moved, transcendentals=0),
            compiler_params=pltpu.CompilerParams(vmem_limit_bytes=24 * 2**20),
        )(*inputs)


def stage_body(source, target, arrived):
    copy = pltpu.make_async_copy(source, target, arrived)
    copy.start()
    copy.wait()


def stage(kernel):
    return pl.pallas_call(
        stage_body,
        in_specs=[pl.BlockSpec(memory_space=pl.ANY)],
        out_specs=VMEM,
        out_shape=jax.ShapeDtypeStruct(kernel.shape, kernel.dtype),
        scratch_shapes=[pltpu.SemaphoreType.DMA],
        cost_estimate=pl.CostEstimate(flops=0, bytes_accessed=4 * kernel.size, transcendentals=0),
        compiler_params=pltpu.CompilerParams(vmem_limit_bytes=24 * 2**20),
    )(kernel)


def join_body(own, came, out):
    core = lax.axis_index("img") % 2
    out[pl.ds(core, 1)] = own[...].reshape((1,) + own.shape)
    out[pl.ds(1 - core, 1)] = came[...].reshape((1,) + came.shape)


def join(plan, own):
    return plan.call(join_body, [own, plan.swap(own, 0)], [((2,) + own.shape, own.dtype)])[0]


def place(plan, rows, frame, row_at, lane_at, wide):
    x = rows.astype(F32)
    column = lax.broadcasted_iota(jnp.int32, x.shape, 0) % plan.width
    left = jnp.where(column == 0, 0.0, pltpu.roll(x, 1, 0))
    right = jnp.where(column == plan.width - 1, 0.0, pltpu.roll(x, x.shape[0] - 1, 0))
    for b, moved in enumerate((left, x, right)):
        wide[frame, pl.ds(row_at, x.shape[0]), pl.ds(b * plan.c_in + lane_at, plan.piece)] = moved.astype(BF16)


def clear_edges(plan, wide):
    zero = jnp.zeros((plan.width, wide.shape[2]), BF16)
    for f in range(wide.shape[0]):
        wide[f, 0 : plan.width, :] = zero
        wide[f, plan.width + plan.pixels :, :] = zero


def times(plan, rows, kernel):
    summed = None
    for a in range(3):
        term = jnp.dot(rows(a), kernel[a].reshape(3 * plan.c_in, plan.c_out), preferred_element_type=F32)
        summed = term if summed is None else summed + term
    return summed


def half_rows(plan, wide, core, a):
    half = plan.pixels // 2
    rows = pl.ds(pl.multiple_of(core * half + a * plan.width, 16), half)
    return wide[:, rows, :].reshape(-1, 3 * plan.c_in)


def one_body(plan, *refs):
    pieces, (kernel, send, keep, wide) = refs[:-4], refs[-4:]
    level, col = where_am_i()
    clear_edges(plan, wide)
    for n, piece in enumerate(pieces):
        place(plan, piece[...], n // plan.ratio, plan.width, plan.lanes(level, n % plan.ratio), wide)
    halves = lambda a: jnp.concatenate([half_rows(plan, wide, core, a) for core in (1 - col % 2, col % 2)], axis=0)
    summed = times(plan, halves, kernel)
    size = summed.shape[0] // 2
    send[...] = summed[:size].astype(BF16).reshape(send.shape)
    keep[...] = summed[size:].reshape(keep.shape)


def conv_one(plan, pieces, kernel):
    frames = len(pieces) // plan.ratio
    half = (frames, plan.pixels // 2, plan.c_out)
    flops = 18 * frames * plan.pixels * plan.c_in * plan.c_out
    outputs = [(half, BF16), (half, F32)]
    scratch = [pltpu.VMEM(plan.wide(frames), BF16)]
    return plan.call(functools.partial(one_body, plan), [*pieces, kernel], outputs, flops, scratch)


def halve_body(bit, kept, came, keep, send):
    half = keep.shape[1]
    mine = (lax.axis_index("img") // 2**bit) % 2 * half
    a = pl.ds(pl.multiple_of(mine, 16), half)
    b = pl.ds(pl.multiple_of(half - mine, 16), half)
    send[...] = (kept[:, b, :] + came[:, b, :].astype(F32)).astype(BF16)
    keep[...] = kept[:, a, :] + came[:, a, :].astype(F32)


def silu_body(kept, came, hidden):
    v = kept[...] + came[...].astype(F32)
    hidden[...] = (v / (1.0 + jnp.exp(-v))).astype(BF16)


def halve(plan, bit, keep, came):
    half = (keep.shape[0], keep.shape[1] // 2, plan.c_out)
    return plan.call(functools.partial(halve_body, bit), [keep, came], [(half, F32), (half, BF16)])


def sum_one(plan, keep, came):
    keep, send = halve(plan, 1, keep, came)
    for bit in range(2, plan.bits):
        keep, send = halve(plan, bit, keep, plan.swap(send, bit - 1))
    return keep, send


def add_silu(plan, keep, came):
    return plan.call(silu_body, [keep, came], [(keep.shape, BF16)])[0]


def conv_two_body(plan, chosen, *refs):
    pieces, (kernel, out, wide) = refs[:-3], refs[-3:]
    level = lax.axis_index("chan")
    clear_edges(plan, wide)
    for n, piece in enumerate(pieces):
        turn, e = n // plan.ratio, n % plan.ratio
        pair = (level // plan.ratio + turn) % plan.pairs
        for core in range(2):
            row_at = pl.multiple_of(plan.width + plan.first_row(2 * pair + core), 16)
            for f, at in enumerate(chosen):
                place(plan, piece[core, at], f, row_at, plan.lanes(level, e), wide)
    rows = lambda a: wide[:, a * plan.width : a * plan.width + plan.pixels, :].reshape(-1, 3 * plan.c_in)
    out[...] = times(plan, rows, kernel).astype(out.dtype).reshape(out.shape)


def conv_two(plan, pieces, chosen, kernel, dtype):
    frames = len(chosen)
    return plan.call(
        functools.partial(conv_two_body, plan, chosen),
        [*pieces, kernel],
        [((frames, plan.pixels, plan.c_out), dtype)],
        18 * frames * plan.pixels * plan.c_in * plan.c_out,
        [pltpu.VMEM(plan.wide(frames), BF16)],
    )[0]


def aligned(bit, came, n):
    low = (lax.axis_index("img") // 2**bit) % 2 == 0
    return jnp.where(low, came[n - 1 if n else came.shape[0] - 1].astype(F32), came[n].astype(F32))


def merge_body(bit, at, kept, came, out):
    for n, t in enumerate(at):
        out[n] = (kept[n].astype(F32) + aligned(bit, came, t)).astype(out.dtype)


def merge(plan, bit, kept, came, at, dtype):
    body = functools.partial(merge_body, bit, at)
    return plan.call(body, [kept, came], [(kept.shape, dtype)])[0]


def last_body(kept, first, came, out):
    out[...] = (kept[...] + aligned(0, first, 0)[None] + came[...].astype(F32)).astype(BF16)


def sum_rest(plan, here, first, send):
    if plan.bits == 2:
        came = plan.swap(send, 1)
        return plan.call(last_body, [here, first, came], [(here.shape, BF16)])[0]
    keep = merge(plan, 0, here, first, range(0, 2 * here.shape[0], 2), F32)
    for bit in range(1, plan.bits):
        came = plan.swap(send, bit)
        count = keep.shape[0]
        total = merge(plan, bit, keep, came, range(count), F32 if count > 1 else BF16)
        keep, send = total[0::2], total[1::2].astype(BF16)
    return total


def shards(mesh, features, kernel_one, kernel_two):
    plan = Plan(mesh, features, kernel_one)
    block = features.reshape(plan.pixels, plan.piece)
    odd = list(range(1, plan.cols, 2))
    even = list(range(2, plan.cols, 4)) + list(range(0, plan.cols, 4))
    early = [p for d in odd for p in plan.spread_frame(block, d)]
    kernel_one = stage(kernel_one)
    late = [p for d in even for p in plan.spread_frame(block, d)]
    last = plan.bits - 1
    send, keep = conv_one(plan, early, kernel_one)
    keep, ahead = sum_one(plan, keep, after(plan.swap(send, 0), late))
    send, kept = conv_one(plan, after(late, ahead), kernel_one)
    hidden = join(plan, add_silu(plan, keep, after(plan.swap(ahead, last), send)))
    odds = [p for t in range(plan.pairs) for p in plan.spread(hidden, t)]
    keep, behind = sum_one(plan, kept, after(plan.swap(send, 0), hidden))
    hidden = join(plan, add_silu(plan, keep, plan.swap(behind, last)))
    evens = [p for t in range(plan.pairs) for p in plan.spread(hidden, t)]
    count = len(odd)
    sums = conv_two(plan, after(odds, hidden), range(count), kernel_two, BF16)
    came = plan.swap(after(sums, evens), 0)
    here = conv_two(plan, evens, range(count // 2), kernel_two, F32)
    send = merge(plan, 0, here, came, range(1, count, 2), BF16)
    here = conv_two(plan, evens, range(count // 2, count), kernel_two, F32)
    return sum_rest(plan, here, came, send).reshape(features.shape)


def solution(mesh):
    placed = (
        P(("groups", "img"), None, None, "chan"),
        P(None, None, "img", "chan"),
        P(None, None, "img", "chan"),
    )
    return jax.shard_map(
        functools.partial(shards, mesh),
        mesh=mesh,
        in_specs=placed,
        out_specs=P(("groups", "img"), None, None, "chan"),
        check_vma=False,
    )
```

```python
import functools

import jax
import jax.numpy as jnp
from jax import lax
from jax.experimental import pallas as pl
from jax.experimental.pallas import tpu as pltpu
from jax.sharding import PartitionSpec as P

VMEM = pl.BlockSpec(memory_space=pltpu.VMEM)
F32, BF16 = jnp.float32, jnp.bfloat16


def where_am_i():
    return lax.axis_index("chan"), lax.axis_index("img")


def after(x, *first):
    return lax.optimization_barrier((x, first))[0]


class Plan:
    def __init__(self, mesh, features, kernel):
        self.levels, self.cols = mesh.shape["chan"], mesh.shape["img"]
        self.pairs, self.ratio = self.cols // 2, self.levels // self.cols
        self.width = features.shape[2]
        self.pixels = features.shape[1] * features.shape[2]
        self.piece = features.shape[3]
        self.c_in, self.c_out = kernel.shape[2], kernel.shape[3]
        self.share = self.pixels // self.cols
        self.bits = self.cols.bit_length() - 1

    def wide(self, frames):
        return (frames, self.pixels + 2 * self.width, 3 * self.c_in)

    def spread_frame(self, x, turn):
        taken = []
        for e in range(self.ratio):
            moves = []
            for k in range(self.levels):
                for f in range(self.cols):
                    level = (f - turn) % self.cols * self.ratio + (k % self.ratio - e) % self.ratio
                    moves.append((k * self.cols + f, level * self.cols + k // self.ratio))
            taken.append(lax.ppermute(x, ("chan", "img"), moves))
        return taken

    def spread(self, x, turn):
        taken = []
        for e in range(self.ratio):
            moves = []
            for level in range(self.levels):
                v, u = level // self.ratio, level % self.ratio
                core, pair = v // self.pairs, (v + turn) % self.pairs
                for col in range(self.cols):
                    source = col * self.ratio + (u + e) % self.ratio
                    moves.append((source * self.cols + 2 * pair + core, level * self.cols + col))
            taken.append(lax.ppermute(x, ("chan", "img"), moves))
        return taken

    def lanes(self, level, e):
        if self.ratio == 1:
            return 0
        return pl.multiple_of((level + e) % self.ratio * self.piece, 128)

    def first_row(self, col):
        at, size = 0, self.pixels
        for bit in range(self.bits):
            size //= 2
            at = at + (col // 2**bit) % 2 * size
        return at

    def swap(self, x, bit):
        return lax.ppermute(x, "img", [(i, i ^ (1 << bit)) for i in range(self.cols)])

    def call(self, body, inputs, outputs, flops=0, scratch=()):
        moved = sum(x.size * x.dtype.itemsize for x in inputs)
        return pl.pallas_call(
            body,
            in_specs=[VMEM] * len(inputs),
            out_specs=[VMEM] * len(outputs),
            out_shape=[jax.ShapeDtypeStruct(*o) for o in outputs],
            scratch_shapes=list(scratch),
            cost_estimate=pl.CostEstimate(flops=flops, bytes_accessed=moved, transcendentals=0),
            compiler_params=pltpu.CompilerParams(vmem_limit_bytes=24 * 2**20),
        )(*inputs)


def stage_body(source, target, arrived):
    copy = pltpu.make_async_copy(source, target, arrived)
    copy.start()
    copy.wait()


def stage(kernel):
    return pl.pallas_call(
        stage_body,
        in_specs=[pl.BlockSpec(memory_space=pl.ANY)],
        out_specs=VMEM,
        out_shape=jax.ShapeDtypeStruct(kernel.shape, kernel.dtype),
        scratch_shapes=[pltpu.SemaphoreType.DMA],
        cost_estimate=pl.CostEstimate(flops=0, bytes_accessed=4 * kernel.size, transcendentals=0),
        compiler_params=pltpu.CompilerParams(vmem_limit_bytes=24 * 2**20),
    )(kernel)


def join_body(own, came, out):
    core = lax.axis_index("img") % 2
    out[pl.ds(core, 1)] = own[...].reshape((1,) + own.shape)
    out[pl.ds(1 - core, 1)] = came[...].reshape((1,) + came.shape)


def join(plan, own):
    return plan.call(join_body, [own, plan.swap(own, 0)], [((2,) + own.shape, own.dtype)])[0]


def place(plan, rows, frame, row_at, lane_at, wide):
    x = rows.astype(F32)
    column = lax.broadcasted_iota(jnp.int32, x.shape, 0) % plan.width
    left = jnp.where(column == 0, 0.0, pltpu.roll(x, 1, 0))
    right = jnp.where(column == plan.width - 1, 0.0, pltpu.roll(x, x.shape[0] - 1, 0))
    for b, moved in enumerate((left, x, right)):
        wide[frame, pl.ds(row_at, x.shape[0]), pl.ds(b * plan.c_in + lane_at, plan.piece)] = moved.astype(BF16)


def clear_edges(plan, wide):
    zero = jnp.zeros((plan.width, wide.shape[2]), BF16)
    for f in range(wide.shape[0]):
        wide[f, 0 : plan.width, :] = zero
        wide[f, plan.width + plan.pixels :, :] = zero


def times(plan, rows, kernel):
    summed = None
    for a in range(3):
        term = jnp.dot(rows(a), kernel[a].reshape(3 * plan.c_in, plan.c_out), preferred_element_type=F32)
        summed = term if summed is None else summed + term
    return summed


def half_rows(plan, wide, core, a):
    half = plan.pixels // 2
    rows = pl.ds(pl.multiple_of(core * half + a * plan.width, 16), half)
    return wide[:, rows, :].reshape(-1, 3 * plan.c_in)


def one_body(plan, *refs):
    frames = refs[-1].shape[0]
    pieces, (kernel, keep, *sends, wide) = refs[: frames * plan.ratio], refs[frames * plan.ratio :]
    level, col = where_am_i()
    clear_edges(plan, wide)
    for n, piece in enumerate(pieces):
        place(plan, piece[...], n // plan.ratio, plan.width, plan.lanes(level, n % plan.ratio), wide)
    halves = lambda a: jnp.concatenate([half_rows(plan, wide, core, a) for core in (1 - col % 2, col % 2)], axis=0)
    summed = times(plan, halves, kernel)
    size = summed.shape[0] // 2
    keep[...] = summed[size:].reshape(keep.shape)
    for n, send in enumerate(sends):
        rows = send.shape[0]
        send[...] = summed[n * rows : (n + 1) * rows].astype(BF16)


def conv_one(plan, pieces, kernel):
    frames = len(pieces) // plan.ratio
    half = (frames, plan.pixels // 2, plan.c_out)
    flops = 18 * frames * plan.pixels * plan.c_in * plan.c_out
    outputs = [(half, F32)] + [(half[1:], BF16)] * frames
    scratch = [pltpu.VMEM(plan.wide(frames), BF16)]
    keep, *sends = plan.call(functools.partial(one_body, plan), [*pieces, kernel], outputs, flops, scratch)
    return keep, [plan.swap(send, 0) for send in sends]


def one_sent_body(plan, *refs):
    frames = refs[-1].shape[0]
    pieces, (kernel, *sends, wide) = refs[: frames * plan.ratio], refs[frames * plan.ratio :]
    level, col = where_am_i()
    clear_edges(plan, wide)
    for n, piece in enumerate(pieces):
        place(plan, piece[...], n // plan.ratio, plan.width, plan.lanes(level, n % plan.ratio), wide)
    summed = times(plan, lambda a: half_rows(plan, wide, 1 - col % 2, a), kernel)
    for n, send in enumerate(sends):
        rows = send.shape[0]
        send[...] = summed[n * rows : (n + 1) * rows].astype(BF16)


def one_kept_body(plan, wide, kernel, keep):
    col = lax.axis_index("img")
    keep[...] = times(plan, lambda a: half_rows(plan, wide, col % 2, a), kernel).reshape(keep.shape)


def conv_one_in_two(plan, pieces, kernel):
    frames = len(pieces) // plan.ratio
    half = (frames, plan.pixels // 2, plan.c_out)
    flops = 9 * frames * plan.pixels * plan.c_in * plan.c_out
    outputs = [(half[1:], BF16)] * frames + [(plan.wide(frames), BF16)]
    *sends, wide = plan.call(functools.partial(one_sent_body, plan), [*pieces, kernel], outputs, flops)
    cames = [plan.swap(send, 0) for send in sends]
    keep = plan.call(functools.partial(one_kept_body, plan), [wide, kernel], [(half, F32)], flops)[0]
    return keep, cames


def halve_body(bit, kept, *refs):
    *cames, keep, send = refs
    half = keep.shape[1]
    mine = (lax.axis_index("img") // 2**bit) % 2 * half
    a = pl.ds(pl.multiple_of(mine, 16), half)
    b = pl.ds(pl.multiple_of(half - mine, 16), half)
    for n, came in enumerate(cames):
        send[n] = (kept[n, b, :] + came[b, :].astype(F32)).astype(BF16)
        keep[n] = kept[n, a, :] + came[a, :].astype(F32)


def silu_body(kept, came, hidden):
    v = kept[...] + came[...].astype(F32)
    hidden[...] = (v / (1.0 + jnp.exp(-v))).astype(BF16)


def halve(plan, bit, keep, cames):
    half = (keep.shape[0], keep.shape[1] // 2, plan.c_out)
    return plan.call(functools.partial(halve_body, bit), [keep, *cames], [(half, F32), (half, BF16)])


def sum_one(plan, keep, cames):
    keep, send = halve(plan, 1, keep, cames)
    for bit in range(2, plan.bits):
        came = plan.swap(send, bit - 1)
        keep, send = halve(plan, bit, keep, [came[n] for n in range(came.shape[0])])
    return keep, send


def add_silu(plan, keep, came):
    return plan.call(silu_body, [keep, came], [(keep.shape, BF16)])[0]


def conv_two_body(plan, chosen, *refs):
    pieces, (kernel, out, wide) = refs[:-3], refs[-3:]
    level = lax.axis_index("chan")
    clear_edges(plan, wide)
    for n, piece in enumerate(pieces):
        turn, e = n // plan.ratio, n % plan.ratio
        pair = (level // plan.ratio + turn) % plan.pairs
        for core in range(2):
            row_at = pl.multiple_of(plan.width + plan.first_row(2 * pair + core), 16)
            for f, at in enumerate(chosen):
                place(plan, piece[core, at], f, row_at, plan.lanes(level, e), wide)
    rows = lambda a: wide[:, a * plan.width : a * plan.width + plan.pixels, :].reshape(-1, 3 * plan.c_in)
    out[...] = times(plan, rows, kernel).astype(out.dtype).reshape(out.shape)


def conv_two(plan, pieces, chosen, kernel, dtype):
    frames = len(chosen)
    return plan.call(
        functools.partial(conv_two_body, plan, chosen),
        [*pieces, kernel],
        [((frames, plan.pixels, plan.c_out), dtype)],
        18 * frames * plan.pixels * plan.c_in * plan.c_out,
        [pltpu.VMEM(plan.wide(frames), BF16)],
    )[0]


def aligned(bit, came, n):
    low = (lax.axis_index("img") // 2**bit) % 2 == 0
    return jnp.where(low, came[n - 1 if n else came.shape[0] - 1].astype(F32), came[n].astype(F32))


def merge_body(bit, at, kept, came, out):
    for n, t in enumerate(at):
        out[n] = (kept[n].astype(F32) + aligned(bit, came, t)).astype(out.dtype)


def merge(plan, bit, kept, came, at, dtype):
    body = functools.partial(merge_body, bit, at)
    return plan.call(body, [kept, came], [(kept.shape, dtype)])[0]


def last_body(kept, first, came, out):
    out[...] = (kept[...] + aligned(0, first, 0)[None] + came[...].astype(F32)).astype(BF16)


def sum_rest(plan, here, first, send):
    if plan.bits == 2:
        came = plan.swap(send, 1)
        return plan.call(last_body, [here, first, came], [(here.shape, BF16)])[0]
    keep = merge(plan, 0, here, first, range(0, 2 * here.shape[0], 2), F32)
    for bit in range(1, plan.bits):
        came = plan.swap(send, bit)
        count = keep.shape[0]
        total = merge(plan, bit, keep, came, range(count), F32 if count > 1 else BF16)
        keep, send = total[0::2], total[1::2].astype(BF16)
    return total


def shards(mesh, features, kernel_one, kernel_two):
    plan = Plan(mesh, features, kernel_one)
    block = features.reshape(plan.pixels, plan.piece)
    odd = list(range(1, plan.cols, 2))
    even = list(range(2, plan.cols, 4)) + list(range(0, plan.cols, 4))
    early = [p for d in odd for p in plan.spread_frame(block, d)]
    kernel_one = stage(kernel_one)
    late = [p for d in even for p in plan.spread_frame(block, d)]
    last = plan.bits - 1
    keep, ahead = sum_one(plan, *conv_one_in_two(plan, early, kernel_one))
    kept, cames = conv_one(plan, after(late, ahead), kernel_one)
    hidden = join(plan, add_silu(plan, keep, after(plan.swap(ahead, last), kept)))
    odds = [p for t in range(plan.pairs) for p in plan.spread(hidden, t)]
    keep, behind = sum_one(plan, kept, after(cames, hidden))
    hidden = join(plan, add_silu(plan, keep, plan.swap(behind, last)))
    evens = [p for t in range(plan.pairs) for p in plan.spread(hidden, t)]
    count = len(odd)
    sums = conv_two(plan, after(odds, hidden), range(count), kernel_two, BF16)
    came = plan.swap(after(sums, evens), 0)
    here = conv_two(plan, evens, range(count // 2), kernel_two, F32)
    send = merge(plan, 0, here, came, range(1, count, 2), BF16)
    here = conv_two(plan, evens, range(count // 2, count), kernel_two, F32)
    return sum_rest(plan, here, came, send).reshape(features.shape)


def solution(mesh):
    placed = (
        P(("groups", "img"), None, None, "chan"),
        P(None, None, "img", "chan"),
        P(None, None, "img", "chan"),
    )
    return jax.shard_map(
        functools.partial(shards, mesh),
        mesh=mesh,
        in_specs=placed,
        out_specs=P(("groups", "img"), None, None, "chan"),
        check_vma=False,
    )
```

```python
import functools

import jax
import jax.numpy as jnp
from jax import lax
from jax.experimental import pallas as pl
from jax.experimental.pallas import tpu as pltpu
from jax.sharding import PartitionSpec as P

VMEM = pl.BlockSpec(memory_space=pltpu.VMEM)
F32, BF16 = jnp.float32, jnp.bfloat16


def where_am_i():
    return lax.axis_index("chan"), lax.axis_index("img")


def after(x, *first):
    return lax.optimization_barrier((x, first))[0]


class Plan:
    def __init__(self, mesh, features, kernel):
        self.levels, self.cols = mesh.shape["chan"], mesh.shape["img"]
        self.pairs, self.ratio = self.cols // 2, self.levels // self.cols
        self.width = features.shape[2]
        self.pixels = features.shape[1] * features.shape[2]
        self.piece = features.shape[3]
        self.c_in, self.c_out = kernel.shape[2], kernel.shape[3]
        self.share = self.pixels // self.cols
        self.bits = self.cols.bit_length() - 1
        self.order = [0, *range(self.bits - 1, 0, -1)]

    def wide(self, frames):
        return (frames, self.pixels + 2 * self.width, 3 * self.c_in)

    def spread_frame(self, x, turn):
        taken = []
        for e in range(self.ratio):
            moves = []
            for k in range(self.levels):
                for f in range(self.cols):
                    level = (f - turn) % self.cols * self.ratio + (k % self.ratio - e) % self.ratio
                    moves.append((k * self.cols + f, level * self.cols + k // self.ratio))
            taken.append(lax.ppermute(x, ("chan", "img"), moves))
        return taken

    def spread(self, x, turn):
        taken = []
        for e in range(self.ratio):
            moves = []
            for level in range(self.levels):
                v, u = level // self.ratio, level % self.ratio
                core, pair = v // self.pairs, (v + turn) % self.pairs
                for col in range(self.cols):
                    source = col * self.ratio + (u + e) % self.ratio
                    moves.append((source * self.cols + 2 * pair + core, level * self.cols + col))
            taken.append(lax.ppermute(x, ("chan", "img"), moves))
        return taken

    def lanes(self, level, e):
        if self.ratio == 1:
            return 0
        return pl.multiple_of((level + e) % self.ratio * self.piece, 128)

    def swap(self, x, bit):
        return lax.ppermute(x, "img", [(i, i ^ (1 << bit)) for i in range(self.cols)])

    def call(self, body, inputs, outputs, flops=0, scratch=()):
        moved = sum(x.size * x.dtype.itemsize for x in inputs)
        return pl.pallas_call(
            body,
            in_specs=[VMEM] * len(inputs),
            out_specs=[VMEM] * len(outputs),
            out_shape=[jax.ShapeDtypeStruct(*o) for o in outputs],
            scratch_shapes=list(scratch),
            cost_estimate=pl.CostEstimate(flops=flops, bytes_accessed=moved, transcendentals=0),
            compiler_params=pltpu.CompilerParams(vmem_limit_bytes=24 * 2**20),
        )(*inputs)


def stage_body(source, target, arrived):
    copy = pltpu.make_async_copy(source, target, arrived)
    copy.start()
    copy.wait()


def stage(kernel):
    return pl.pallas_call(
        stage_body,
        in_specs=[pl.BlockSpec(memory_space=pl.ANY)],
        out_specs=VMEM,
        out_shape=jax.ShapeDtypeStruct(kernel.shape, kernel.dtype),
        scratch_shapes=[pltpu.SemaphoreType.DMA],
        cost_estimate=pl.CostEstimate(flops=0, bytes_accessed=4 * kernel.size, transcendentals=0),
        compiler_params=pltpu.CompilerParams(vmem_limit_bytes=24 * 2**20),
    )(kernel)


def join_body(own, came, out):
    core = lax.axis_index("img") % 2
    out[pl.ds(core, 1)] = own[...].reshape((1,) + own.shape)
    out[pl.ds(1 - core, 1)] = came[...].reshape((1,) + came.shape)


def join(plan, own):
    return plan.call(join_body, [own, plan.swap(own, 0)], [((2,) + own.shape, own.dtype)])[0]


def place(plan, rows, frame, row_at, lane_at, wide):
    x = rows.astype(F32)
    column = lax.broadcasted_iota(jnp.int32, x.shape, 0) % plan.width
    left = jnp.where(column == 0, 0.0, pltpu.roll(x, 1, 0))
    right = jnp.where(column == plan.width - 1, 0.0, pltpu.roll(x, x.shape[0] - 1, 0))
    for b, moved in enumerate((left, x, right)):
        wide[frame, pl.ds(row_at, x.shape[0]), pl.ds(b * plan.c_in + lane_at, plan.piece)] = moved.astype(BF16)


def clear_edges(plan, wide):
    zero = jnp.zeros((plan.width, wide.shape[2]), BF16)
    for f in range(wide.shape[0]):
        wide[f, 0 : plan.width, :] = zero
        wide[f, plan.width + plan.pixels :, :] = zero


def times(plan, rows, kernel):
    summed = None
    for a in range(3):
        term = jnp.dot(rows(a), kernel[a].reshape(3 * plan.c_in, plan.c_out), preferred_element_type=F32)
        summed = term if summed is None else summed + term
    return summed


def half_rows(plan, wide, core, a):
    blocks = []
    for f in range(wide.shape[0]):
        for pair in range(plan.pairs):
            start = (2 * pair + core) * plan.share + a * plan.width
            blocks.append(wide[f, pl.ds(pl.multiple_of(start, 16), plan.share), :])
    return jnp.concatenate(blocks, axis=0)


def one_body(plan, *refs):
    frames = refs[-1].shape[0]
    pieces, (kernel, keep, *sends, wide) = refs[: frames * plan.ratio], refs[frames * plan.ratio :]
    level, col = where_am_i()
    clear_edges(plan, wide)
    for n, piece in enumerate(pieces):
        place(plan, piece[...], n // plan.ratio, plan.width, plan.lanes(level, n % plan.ratio), wide)
    halves = lambda a: jnp.concatenate([half_rows(plan, wide, core, a) for core in (1 - col % 2, col % 2)], axis=0)
    summed = times(plan, halves, kernel)
    size = summed.shape[0] // 2
    keep[...] = summed[size:].reshape(keep.shape)
    for n, send in enumerate(sends):
        rows = send.shape[0]
        send[...] = summed[n * rows : (n + 1) * rows].astype(BF16)


def conv_one(plan, pieces, kernel):
    frames = len(pieces) // plan.ratio
    half = (frames, plan.pixels // 2, plan.c_out)
    flops = 18 * frames * plan.pixels * plan.c_in * plan.c_out
    outputs = [(half, F32)] + [(half[1:], BF16)] * frames
    scratch = [pltpu.VMEM(plan.wide(frames), BF16)]
    keep, *sends = plan.call(functools.partial(one_body, plan), [*pieces, kernel], outputs, flops, scratch)
    return keep, [plan.swap(send, 0) for send in sends]


def one_sent_body(plan, *refs):
    frames = refs[-1].shape[0]
    pieces, (kernel, *sends, wide) = refs[: frames * plan.ratio], refs[frames * plan.ratio :]
    level, col = where_am_i()
    clear_edges(plan, wide)
    for n, piece in enumerate(pieces):
        place(plan, piece[...], n // plan.ratio, plan.width, plan.lanes(level, n % plan.ratio), wide)
    summed = times(plan, lambda a: half_rows(plan, wide, 1 - col % 2, a), kernel)
    for n, send in enumerate(sends):
        rows = send.shape[0]
        send[...] = summed[n * rows : (n + 1) * rows].astype(BF16)


def one_kept_body(plan, wide, kernel, keep):
    col = lax.axis_index("img")
    keep[...] = times(plan, lambda a: half_rows(plan, wide, col % 2, a), kernel).reshape(keep.shape)


def conv_one_in_two(plan, pieces, kernel):
    frames = len(pieces) // plan.ratio
    half = (frames, plan.pixels // 2, plan.c_out)
    flops = 9 * frames * plan.pixels * plan.c_in * plan.c_out
    outputs = [(half[1:], BF16)] * frames + [(plan.wide(frames), BF16)]
    *sends, wide = plan.call(functools.partial(one_sent_body, plan), [*pieces, kernel], outputs, flops)
    cames = [plan.swap(send, 0) for send in sends]
    keep = plan.call(functools.partial(one_kept_body, plan), [wide, kernel], [(half, F32)], flops)[0]
    return keep, cames


def halve_body(bit, kept, *refs):
    *cames, keep, send = refs
    half = keep.shape[1]
    mine = (lax.axis_index("img") // 2**bit) % 2 * half
    a = pl.ds(pl.multiple_of(mine, 16), half)
    b = pl.ds(pl.multiple_of(half - mine, 16), half)
    for n, came in enumerate(cames):
        send[n] = (kept[n, b, :] + came[b, :].astype(F32)).astype(BF16)
        keep[n] = kept[n, a, :] + came[a, :].astype(F32)


def silu_body(kept, came, hidden):
    v = kept[...] + came[...].astype(F32)
    hidden[...] = (v / (1.0 + jnp.exp(-v))).astype(BF16)


def halve(plan, bit, keep, cames):
    half = (keep.shape[0], keep.shape[1] // 2, plan.c_out)
    return plan.call(functools.partial(halve_body, bit), [keep, *cames], [(half, F32), (half, BF16)])


def sum_one(plan, keep, cames):
    keep, send = halve(plan, plan.order[1], keep, cames)
    for n in range(2, plan.bits):
        came = plan.swap(send, plan.order[n - 1])
        keep, send = halve(plan, plan.order[n], keep, [came[f] for f in range(came.shape[0])])
    return keep, send


def add_silu(plan, keep, came):
    return plan.call(silu_body, [keep, came], [(keep.shape, BF16)])[0]


def conv_two_body(plan, chosen, *refs):
    pieces, (kernel, out, wide) = refs[:-3], refs[-3:]
    level = lax.axis_index("chan")
    clear_edges(plan, wide)
    for n, piece in enumerate(pieces):
        turn, e = n // plan.ratio, n % plan.ratio
        pair = (level // plan.ratio + turn) % plan.pairs
        for core in range(2):
            row_at = pl.multiple_of(plan.width + (2 * pair + core) * plan.share, 16)
            for f, at in enumerate(chosen):
                place(plan, piece[core, at], f, row_at, plan.lanes(level, e), wide)
    rows = lambda a: wide[:, a * plan.width : a * plan.width + plan.pixels, :].reshape(-1, 3 * plan.c_in)
    out[...] = times(plan, rows, kernel).astype(out.dtype).reshape(out.shape)


def conv_two(plan, pieces, chosen, kernel, dtype):
    frames = len(chosen)
    return plan.call(
        functools.partial(conv_two_body, plan, chosen),
        [*pieces, kernel],
        [((frames, plan.pixels, plan.c_out), dtype)],
        18 * frames * plan.pixels * plan.c_in * plan.c_out,
        [pltpu.VMEM(plan.wide(frames), BF16)],
    )[0]


def conv_for_other(plan, pieces, first, kernel, parts):
    return plan.call(
        functools.partial(for_other_body, plan, first),
        [*pieces, kernel],
        [((plan.pixels // parts, plan.c_out), BF16)] * parts,
        18 * plan.pixels * plan.c_in * plan.c_out,
        [pltpu.VMEM(plan.wide(1), BF16)],
    )


def for_other_body(plan, first, *refs):
    count = plan.pairs * plan.ratio
    pieces, kernel, outs, wide = refs[:count], refs[count], refs[count + 1 : -1], refs[-1]
    level, col = where_am_i()
    clear_edges(plan, wide)
    for n, piece in enumerate(pieces):
        turn, e = n // plan.ratio, n % plan.ratio
        pair = (level // plan.ratio + turn) % plan.pairs
        for core in range(2):
            row_at = pl.multiple_of(plan.width + (2 * pair + core) * plan.share, 16)
            place(plan, piece[core, (col + first) % 2], 0, row_at, plan.lanes(level, e), wide)
    total = times(plan, lambda a: wide[0, a * plan.width : a * plan.width + plan.pixels, :], kernel)
    size = plan.pixels // len(outs)
    for n, out in enumerate(outs):
        out[...] = total[n * size : (n + 1) * size].astype(BF16)


def aligned(bit, came, n):
    low = (lax.axis_index("img") // 2**bit) % 2 == 0
    return jnp.where(low, came[n - 1 if n else came.shape[0] - 1].astype(F32), came[n].astype(F32))


def merge_body(bit, at, kept, came, out):
    for n, t in enumerate(at):
        out[n] = (kept[n].astype(F32) + aligned(bit, came, t)).astype(out.dtype)


def merge(plan, bit, kept, came, at, dtype):
    body = functools.partial(merge_body, bit, at)
    return plan.call(body, [kept, came], [(kept.shape, dtype)])[0]


def last_body(kept, first, came, out):
    out[...] = (kept[...] + aligned(0, first, 0)[None] + came[...].astype(F32)).astype(BF16)


def sum_rest(plan, here, first, send):
    if plan.bits == 2:
        came = plan.swap(send, 1)
        return plan.call(last_body, [here, first, came], [(here.shape, BF16)])[0]
    keep = merge(plan, 0, here, first, range(0, 2 * here.shape[0], 2), F32)
    for bit in range(1, plan.bits):
        came = plan.swap(send, bit)
        count = keep.shape[0]
        total = merge(plan, bit, keep, came, range(count), F32 if count > 1 else BF16)
        keep, send = total[0::2], total[1::2].astype(BF16)
    return total


def part_of(plan, part):
    first = lax.axis_index("chan") // plan.ratio % plan.pairs == 0
    size = plan.pixels // 2 - plan.width
    if part == 0:
        return jnp.where(first, 0, plan.pixels - size), size
    if part == 1:
        return jnp.where(first, size, 0), plan.pixels - size
    return 0, plan.pixels


def part_body(plan, part, frame, turns, *refs):
    count = turns * plan.ratio
    pieces, kernel, cames, (out, wide, added) = refs[:count], refs[count], refs[count + 1 : -3], refs[-3:]
    level, col = where_am_i()
    clear_edges(plan, wide)
    for n, piece in enumerate(pieces):
        turn, e = n // plan.ratio, n % plan.ratio
        pair = (level // plan.ratio + turn) % plan.pairs
        for core in range(2):
            row_at = pl.multiple_of(plan.width + (2 * pair + core) * plan.share, 16)
            place(plan, piece[core, frame], 0, row_at, plan.lanes(level, e), wide)
    for n, came in enumerate(cames):
        added[n * came.shape[0] : (n + 1) * came.shape[0], :] = came[...]
    start, size = part_of(plan, part)
    at = lambda a: pl.ds(pl.multiple_of(start + a * plan.width, 16), size)
    total = times(plan, lambda a: wide[0, at(a), :], kernel)
    out[...] = (total + added[at(0), :].astype(F32)).astype(out.dtype)


def conv_part(plan, part, frame, pieces, kernel, cames, dtype):
    size = [plan.pixels // 2 - plan.width, plan.pixels // 2 + plan.width, plan.pixels][part]
    return plan.call(
        functools.partial(part_body, plan, part, frame, len(pieces) // plan.ratio),
        [*pieces, kernel, *cames],
        [((size, plan.c_out), dtype)],
        18 * size * plan.c_in * plan.c_out,
        [pltpu.VMEM(plan.wide(1), BF16), pltpu.VMEM((plan.pixels, plan.c_out), BF16)],
    )[0]


def put_body(plan, kept, *refs):
    *cames, out = refs
    for part, came in enumerate(cames):
        start, size = part_of(plan, part)
        rows = pl.ds(pl.multiple_of(start, 16), size)
        out[rows, :] = (kept[rows, :] + came[...].astype(F32)).astype(BF16)


def sum_in_parts(plan, odds, evens, hidden, kernel):
    odds = after(odds, hidden)
    frames = len(odds[0][0])
    if plan.pairs != 2:
        sums = conv_two(plan, odds, range(frames), kernel, BF16)
        came = plan.swap(after(sums, evens), 0)
        here = conv_two(plan, evens, range(frames // 2), kernel, F32)
        send = merge(plan, 0, here, came, range(1, frames, 2), BF16)
        here = conv_two(plan, evens, range(frames // 2, frames), kernel, F32)
        return sum_rest(plan, here, came, send)
    cames = [plan.swap(part, 0) for part in conv_for_other(plan, odds, 1, kernel, 2)]
    own = conv_for_other(plan, odds, 0, kernel, 1)[0]
    near, both = after(evens[: plan.ratio], own), evens
    sums = conv_part(plan, 0, 0, near, kernel, cames, BF16)
    early = plan.swap(sums, 1)
    sums = conv_part(plan, 1, 0, after(both, sums), kernel, cames, BF16)
    late = plan.swap(sums, 1)
    early = after(early, sums)
    kept = conv_part(plan, 2, 1, after(both, early), kernel, [plan.swap(own, 0)], F32)
    body = functools.partial(put_body, plan)
    return plan.call(body, [kept, early, late], [(kept.shape, BF16)])[0]


def shards(mesh, features, kernel_one, kernel_two):
    plan = Plan(mesh, features, kernel_one)
    block = features.reshape(plan.pixels, plan.piece)
    odd = list(range(1, plan.cols, 2))
    even = list(range(2, plan.cols, 4)) + list(range(0, plan.cols, 4))
    early = [p for d in odd for p in plan.spread_frame(block, d)]
    kernel_one = stage(kernel_one)
    late = [p for d in even for p in plan.spread_frame(block, d)]
    last = plan.order[-1]
    keep, ahead = sum_one(plan, *conv_one_in_two(plan, early, kernel_one))
    kept, cames = conv_one(plan, after(late, ahead), kernel_one)
    hidden = join(plan, add_silu(plan, keep, after(plan.swap(ahead, last), kept)))
    odds = [p for t in range(plan.pairs) for p in plan.spread(hidden, t)]
    keep, behind = sum_one(plan, kept, after(cames, hidden))
    hidden = join(plan, add_silu(plan, keep, plan.swap(behind, last)))
    evens = [p for t in range(plan.pairs) for p in plan.spread(hidden, t)]
    return sum_in_parts(plan, odds, evens, hidden, kernel_two).reshape(features.shape)


def solution(mesh):
    placed = (
        P(("groups", "img"), None, None, "chan"),
        P(None, None, "img", "chan"),
        P(None, None, "img", "chan"),
    )
    return jax.shard_map(
        functools.partial(shards, mesh),
        mesh=mesh,
        in_specs=placed,
        out_specs=P(("groups", "img"), None, None, "chan"),
        check_vma=False,
    )
```

```python
import functools

import jax
import jax.numpy as jnp
from jax import lax
from jax.experimental import pallas as pl
from jax.experimental.pallas import tpu as pltpu
from jax.sharding import PartitionSpec as P

VMEM = pl.BlockSpec(memory_space=pltpu.VMEM)
F32, BF16 = jnp.float32, jnp.bfloat16


def where_am_i():
    return lax.axis_index("chan"), lax.axis_index("img")


def after(x, *first):
    return lax.optimization_barrier((x, first))[0]


class Plan:
    def __init__(self, mesh, features, kernel):
        self.levels, self.cols = mesh.shape["chan"], mesh.shape["img"]
        self.pairs, self.ratio = self.cols // 2, self.levels // self.cols
        self.width = features.shape[2]
        self.pixels = features.shape[1] * features.shape[2]
        self.piece = features.shape[3]
        self.c_in, self.c_out = kernel.shape[2], kernel.shape[3]
        self.share = self.pixels // self.cols
        self.bits = self.cols.bit_length() - 1
        self.order = [0, *range(self.bits - 1, 0, -1)]

    def wide(self, frames):
        return (frames, self.pixels + 2 * self.width, 3 * self.c_in)

    def spread_frame(self, x, turn):
        taken = []
        for e in range(self.ratio):
            moves = []
            for k in range(self.levels):
                for f in range(self.cols):
                    level = (f - turn) % self.cols * self.ratio + (k % self.ratio - e) % self.ratio
                    moves.append((k * self.cols + f, level * self.cols + k // self.ratio))
            taken.append(lax.ppermute(x, ("chan", "img"), moves))
        return taken

    def spread(self, x, turn):
        taken = []
        for e in range(self.ratio):
            moves = []
            for level in range(self.levels):
                v, u = level // self.ratio, level % self.ratio
                core, pair = v // self.pairs, (v + turn) % self.pairs
                for col in range(self.cols):
                    source = col * self.ratio + (u + e) % self.ratio
                    moves.append((source * self.cols + 2 * pair + core, level * self.cols + col))
            taken.append(lax.ppermute(x, ("chan", "img"), moves))
        return taken

    def lanes(self, level, e):
        if self.ratio == 1:
            return 0
        return pl.multiple_of((level + e) % self.ratio * self.piece, 128)

    def swap(self, x, bit):
        return lax.ppermute(x, "img", [(i, i ^ (1 << bit)) for i in range(self.cols)])

    def call(self, body, inputs, outputs, flops=0, scratch=()):
        moved = sum(x.size * x.dtype.itemsize for x in inputs)
        return pl.pallas_call(
            body,
            in_specs=[VMEM] * len(inputs),
            out_specs=[VMEM] * len(outputs),
            out_shape=[jax.ShapeDtypeStruct(*o) for o in outputs],
            scratch_shapes=list(scratch),
            cost_estimate=pl.CostEstimate(flops=flops, bytes_accessed=moved, transcendentals=0),
            compiler_params=pltpu.CompilerParams(vmem_limit_bytes=24 * 2**20),
        )(*inputs)


def stage_body(source, target, arrived):
    copy = pltpu.make_async_copy(source, target, arrived)
    copy.start()
    copy.wait()


def stage(kernel):
    return pl.pallas_call(
        stage_body,
        in_specs=[pl.BlockSpec(memory_space=pl.ANY)],
        out_specs=VMEM,
        out_shape=jax.ShapeDtypeStruct(kernel.shape, kernel.dtype),
        scratch_shapes=[pltpu.SemaphoreType.DMA],
        cost_estimate=pl.CostEstimate(flops=0, bytes_accessed=4 * kernel.size, transcendentals=0),
        compiler_params=pltpu.CompilerParams(vmem_limit_bytes=24 * 2**20),
    )(kernel)


def join_body(own, came, out):
    core = lax.axis_index("img") % 2
    out[pl.ds(core, 1)] = own[...].reshape((1,) + own.shape)
    out[pl.ds(1 - core, 1)] = came[...].reshape((1,) + came.shape)


def join(plan, own):
    return plan.call(join_body, [own, plan.swap(own, 0)], [((2,) + own.shape, own.dtype)])[0]


def place(plan, rows, frame, row_at, lane_at, wide):
    x = rows.astype(F32)
    column = lax.broadcasted_iota(jnp.int32, x.shape, 0) % plan.width
    left = jnp.where(column == 0, 0.0, pltpu.roll(x, 1, 0))
    right = jnp.where(column == plan.width - 1, 0.0, pltpu.roll(x, x.shape[0] - 1, 0))
    for b, moved in enumerate((left, x, right)):
        wide[frame, pl.ds(row_at, x.shape[0]), pl.ds(b * plan.c_in + lane_at, plan.piece)] = moved.astype(BF16)


def clear_edges(plan, wide):
    zero = jnp.zeros((plan.width, wide.shape[2]), BF16)
    for f in range(wide.shape[0]):
        wide[f, 0 : plan.width, :] = zero
        wide[f, plan.width + plan.pixels :, :] = zero


def times(plan, rows, kernel):
    summed = None
    for a in range(3):
        term = jnp.dot(rows(a), kernel[a].reshape(3 * plan.c_in, plan.c_out), preferred_element_type=F32)
        summed = term if summed is None else summed + term
    return summed


def half_rows(plan, wide, core, a):
    blocks = []
    for f in range(wide.shape[0]):
        for pair in range(plan.pairs):
            start = (2 * pair + core) * plan.share + a * plan.width
            blocks.append(wide[f, pl.ds(pl.multiple_of(start, 16), plan.share), :])
    return jnp.concatenate(blocks, axis=0)


def one_sent_body(plan, *refs):
    frames = refs[-1].shape[0]
    pieces, (kernel, *sends, wide) = refs[: frames * plan.ratio], refs[frames * plan.ratio :]
    level, col = where_am_i()
    clear_edges(plan, wide)
    for n, piece in enumerate(pieces):
        place(plan, piece[...], n // plan.ratio, plan.width, plan.lanes(level, n % plan.ratio), wide)
    summed = times(plan, lambda a: half_rows(plan, wide, 1 - col % 2, a), kernel)
    for n, send in enumerate(sends):
        rows = send.shape[0]
        send[...] = summed[n * rows : (n + 1) * rows].astype(BF16)


def one_kept_body(plan, wide, kernel, keep):
    col = lax.axis_index("img")
    keep[...] = times(plan, lambda a: half_rows(plan, wide, col % 2, a), kernel).reshape(keep.shape)


def conv_one_in_two(plan, pieces, kernel, parts):
    frames = len(pieces) // plan.ratio
    half = (frames, plan.pixels // 2, plan.c_out)
    flops = 9 * frames * plan.pixels * plan.c_in * plan.c_out
    outputs = [((half[1] // parts, half[2]), BF16)] * (frames * parts) + [(plan.wide(frames), BF16)]
    *sends, wide = plan.call(functools.partial(one_sent_body, plan), [*pieces, kernel], outputs, flops)
    cames = [plan.swap(send, 0) for send in sends]
    keep = plan.call(functools.partial(one_kept_body, plan), [wide, kernel], [(half, F32)], flops)[0]
    return keep, cames


def halve_body(bit, kept, *refs):
    *cames, keep, send = refs
    frames, half = keep.shape[0], keep.shape[1]
    low = (lax.axis_index("img") // 2**bit) % 2 == 0
    mine = jnp.where(low, 0, half)
    a = pl.ds(pl.multiple_of(mine, 16), half)
    b = pl.ds(pl.multiple_of(half - mine, 16), half)
    for n in range(frames):
        if len(cames) == frames:
            mine_came, other_came = cames[n][a, :], cames[n][b, :]
        else:
            first, second = cames[2 * n][...], cames[2 * n + 1][...]
            mine_came, other_came = jnp.where(low, first, second), jnp.where(low, second, first)
        send[n] = (kept[n, b, :] + other_came.astype(F32)).astype(BF16)
        keep[n] = kept[n, a, :] + mine_came.astype(F32)


def silu_body(kept, came, hidden):
    v = kept[...] + came[...].astype(F32)
    hidden[...] = (v / (1.0 + jnp.exp(-v))).astype(BF16)


def halve(plan, bit, keep, cames):
    half = (keep.shape[0], keep.shape[1] // 2, plan.c_out)
    return plan.call(functools.partial(halve_body, bit), [keep, *cames], [(half, F32), (half, BF16)])


def sum_one(plan, keep, cames):
    keep, send = halve(plan, plan.order[1], keep, cames)
    for n in range(2, plan.bits):
        came = plan.swap(send, plan.order[n - 1])
        keep, send = halve(plan, plan.order[n], keep, [came[f] for f in range(came.shape[0])])
    return keep, send


def add_silu(plan, keep, came):
    return plan.call(silu_body, [keep, came], [(keep.shape, BF16)])[0]


def conv_two_body(plan, chosen, *refs):
    pieces, (kernel, out, wide) = refs[:-3], refs[-3:]
    level = lax.axis_index("chan")
    clear_edges(plan, wide)
    for n, piece in enumerate(pieces):
        turn, e = n // plan.ratio, n % plan.ratio
        pair = (level // plan.ratio + turn) % plan.pairs
        for core in range(2):
            row_at = pl.multiple_of(plan.width + (2 * pair + core) * plan.share, 16)
            for f, at in enumerate(chosen):
                place(plan, piece[core, at], f, row_at, plan.lanes(level, e), wide)
    rows = lambda a: wide[:, a * plan.width : a * plan.width + plan.pixels, :].reshape(-1, 3 * plan.c_in)
    out[...] = times(plan, rows, kernel).astype(out.dtype).reshape(out.shape)


def conv_two(plan, pieces, chosen, kernel, dtype):
    frames = len(chosen)
    return plan.call(
        functools.partial(conv_two_body, plan, chosen),
        [*pieces, kernel],
        [((frames, plan.pixels, plan.c_out), dtype)],
        18 * frames * plan.pixels * plan.c_in * plan.c_out,
        [pltpu.VMEM(plan.wide(frames), BF16)],
    )[0]


def conv_for_other(plan, pieces, first, kernel, parts):
    return plan.call(
        functools.partial(for_other_body, plan, first),
        [*pieces, kernel],
        [((plan.pixels // parts, plan.c_out), BF16)] * parts,
        18 * plan.pixels * plan.c_in * plan.c_out,
        [pltpu.VMEM(plan.wide(1), BF16)],
    )


def for_other_body(plan, first, *refs):
    count = plan.pairs * plan.ratio
    pieces, kernel, outs, wide = refs[:count], refs[count], refs[count + 1 : -1], refs[-1]
    level, col = where_am_i()
    clear_edges(plan, wide)
    for n, piece in enumerate(pieces):
        turn, e = n // plan.ratio, n % plan.ratio
        pair = (level // plan.ratio + turn) % plan.pairs
        for core in range(2):
            row_at = pl.multiple_of(plan.width + (2 * pair + core) * plan.share, 16)
            place(plan, piece[core, (col + first) % 2], 0, row_at, plan.lanes(level, e), wide)
    total = times(plan, lambda a: wide[0, a * plan.width : a * plan.width + plan.pixels, :], kernel)
    size = plan.pixels // len(outs)
    for n, out in enumerate(outs):
        out[...] = total[n * size : (n + 1) * size].astype(BF16)


def aligned(bit, came, n):
    low = (lax.axis_index("img") // 2**bit) % 2 == 0
    return jnp.where(low, came[n - 1 if n else came.shape[0] - 1].astype(F32), came[n].astype(F32))


def merge_body(bit, at, kept, came, out):
    for n, t in enumerate(at):
        out[n] = (kept[n].astype(F32) + aligned(bit, came, t)).astype(out.dtype)


def merge(plan, bit, kept, came, at, dtype):
    body = functools.partial(merge_body, bit, at)
    return plan.call(body, [kept, came], [(kept.shape, dtype)])[0]


def last_body(kept, first, came, out):
    out[...] = (kept[...] + aligned(0, first, 0)[None] + came[...].astype(F32)).astype(BF16)


def sum_rest(plan, here, first, send):
    if plan.bits == 2:
        came = plan.swap(send, 1)
        return plan.call(last_body, [here, first, came], [(here.shape, BF16)])[0]
    keep = merge(plan, 0, here, first, range(0, 2 * here.shape[0], 2), F32)
    for bit in range(1, plan.bits):
        came = plan.swap(send, bit)
        count = keep.shape[0]
        total = merge(plan, bit, keep, came, range(count), F32 if count > 1 else BF16)
        keep, send = total[0::2], total[1::2].astype(BF16)
    return total


def part_of(plan, part):
    first = lax.axis_index("chan") // plan.ratio % plan.pairs == 0
    size = plan.pixels // 2 - plan.width
    if part == 0:
        return jnp.where(first, 0, plan.pixels - size), size
    if part == 1:
        return jnp.where(first, size, 0), plan.pixels - size
    return 0, plan.pixels


def part_body(plan, part, frame, turns, *refs):
    count = turns * plan.ratio
    pieces, kernel, cames, (out, wide, added) = refs[:count], refs[count], refs[count + 1 : -3], refs[-3:]
    level, col = where_am_i()
    clear_edges(plan, wide)
    for n, piece in enumerate(pieces):
        turn, e = n // plan.ratio, n % plan.ratio
        pair = (level // plan.ratio + turn) % plan.pairs
        for core in range(2):
            row_at = pl.multiple_of(plan.width + (2 * pair + core) * plan.share, 16)
            place(plan, piece[core, frame], 0, row_at, plan.lanes(level, e), wide)
    for n, came in enumerate(cames):
        added[n * came.shape[0] : (n + 1) * came.shape[0], :] = came[...]
    start, size = part_of(plan, part)
    at = lambda a: pl.ds(pl.multiple_of(start + a * plan.width, 16), size)
    total = times(plan, lambda a: wide[0, at(a), :], kernel)
    out[...] = (total + added[at(0), :].astype(F32)).astype(out.dtype)


def conv_part(plan, part, frame, pieces, kernel, cames, dtype):
    size = [plan.pixels // 2 - plan.width, plan.pixels // 2 + plan.width, plan.pixels][part]
    return plan.call(
        functools.partial(part_body, plan, part, frame, len(pieces) // plan.ratio),
        [*pieces, kernel, *cames],
        [((size, plan.c_out), dtype)],
        18 * size * plan.c_in * plan.c_out,
        [pltpu.VMEM(plan.wide(1), BF16), pltpu.VMEM((plan.pixels, plan.c_out), BF16)],
    )[0]


def put_body(plan, kept, *refs):
    *cames, out = refs
    for part, came in enumerate(cames):
        start, size = part_of(plan, part)
        rows = pl.ds(pl.multiple_of(start, 16), size)
        out[rows, :] = (kept[rows, :] + came[...].astype(F32)).astype(BF16)


def sum_in_parts(plan, odds, evens, hidden, kernel):
    odds = after(odds, hidden)
    frames = len(odds[0][0])
    if plan.pairs != 2:
        sums = conv_two(plan, odds, range(frames), kernel, BF16)
        came = plan.swap(after(sums, evens), 0)
        here = conv_two(plan, evens, range(frames // 2), kernel, F32)
        send = merge(plan, 0, here, came, range(1, frames, 2), BF16)
        here = conv_two(plan, evens, range(frames // 2, frames), kernel, F32)
        return sum_rest(plan, here, came, send)
    cames = [plan.swap(part, 0) for part in conv_for_other(plan, odds, 1, kernel, 2)]
    own = conv_for_other(plan, odds, 0, kernel, 1)[0]
    near, both = after(evens[: plan.ratio], own), evens
    sums = conv_part(plan, 0, 0, near, kernel, cames, BF16)
    early = plan.swap(sums, 1)
    sums = conv_part(plan, 1, 0, after(both, sums), kernel, cames, BF16)
    late = plan.swap(sums, 1)
    early = after(early, sums)
    kept = conv_part(plan, 2, 1, after(both, early), kernel, [plan.swap(own, 0)], F32)
    body = functools.partial(put_body, plan)
    return plan.call(body, [kept, early, late], [(kept.shape, BF16)])[0]


def shards(mesh, features, kernel_one, kernel_two):
    plan = Plan(mesh, features, kernel_one)
    block = features.reshape(plan.pixels, plan.piece)
    odd = list(range(1, plan.cols, 2))
    even = list(range(2, plan.cols, 4)) + list(range(0, plan.cols, 4))
    early = [p for d in odd for p in plan.spread_frame(block, d)]
    kernel_one = stage(kernel_one)
    late = [p for d in even for p in plan.spread_frame(block, d)]
    last = plan.order[-1]
    keep, ahead = sum_one(plan, *conv_one_in_two(plan, early, kernel_one, 1))
    kept, cames = conv_one_in_two(plan, after(late, ahead), kernel_one, 2)
    kept, behind = sum_one(plan, kept, cames)
    hidden = join(plan, add_silu(plan, keep, after(plan.swap(ahead, last), behind)))
    odds = [p for t in range(plan.pairs) for p in plan.spread(hidden, t)]
    hidden = join(plan, add_silu(plan, kept, plan.swap(behind, last)))
    evens = [p for t in range(plan.pairs) for p in plan.spread(hidden, t)]
    return sum_in_parts(plan, odds, evens, hidden, kernel_two).reshape(features.shape)


def solution(mesh):
    placed = (
        P(("groups", "img"), None, None, "chan"),
        P(None, None, "img", "chan"),
        P(None, None, "img", "chan"),
    )
    return jax.shard_map(
        functools.partial(shards, mesh),
        mesh=mesh,
        in_specs=placed,
        out_specs=P(("groups", "img"), None, None, "chan"),
        check_vma=False,
    )
```

```python
import functools

import jax
import jax.numpy as jnp
from jax import lax
from jax.experimental import pallas as pl
from jax.experimental.pallas import tpu as pltpu
from jax.sharding import PartitionSpec as P

VMEM = pl.BlockSpec(memory_space=pltpu.VMEM)
F32, BF16 = jnp.float32, jnp.bfloat16


def where_am_i():
    return lax.axis_index("chan"), lax.axis_index("img")


def after(x, *first):
    return lax.optimization_barrier((x, first))[0]


class Plan:
    def __init__(self, mesh, features, kernel):
        self.levels, self.cols = mesh.shape["chan"], mesh.shape["img"]
        self.pairs, self.ratio = self.cols // 2, self.levels // self.cols
        self.width = features.shape[2]
        self.pixels = features.shape[1] * features.shape[2]
        self.piece = features.shape[3]
        self.c_in, self.c_out = kernel.shape[2], kernel.shape[3]
        self.share = self.pixels // self.cols
        self.bits = self.cols.bit_length() - 1
        self.order = [0, *range(self.bits - 1, 0, -1)]

    def wide(self, frames):
        return (frames, self.pixels + 2 * self.width, 3 * self.c_in)

    def spread_frame(self, x, turn):
        taken = []
        for e in range(self.ratio):
            moves = []
            for k in range(self.levels):
                for f in range(self.cols):
                    level = (f - turn) % self.cols * self.ratio + (k % self.ratio - e) % self.ratio
                    moves.append((k * self.cols + f, level * self.cols + k // self.ratio))
            taken.append(lax.ppermute(x, ("chan", "img"), moves))
        return taken

    def spread(self, x, turn):
        taken = []
        for e in range(self.ratio):
            moves = []
            for level in range(self.levels):
                v, u = level // self.ratio, level % self.ratio
                core = v // self.pairs
                for col in range(self.cols):
                    pair = (v + col + turn) % self.pairs
                    source = col * self.ratio + (u + e) % self.ratio
                    moves.append((source * self.cols + 2 * pair + core, level * self.cols + col))
            taken.append(lax.ppermute(x, ("chan", "img"), moves))
        return taken

    def lanes(self, level, e):
        if self.ratio == 1:
            return 0
        return pl.multiple_of((level + e) % self.ratio * self.piece, 128)

    def swap(self, x, bit):
        return lax.ppermute(x, "img", [(i, i ^ (1 << bit)) for i in range(self.cols)])

    def call(self, body, inputs, outputs, flops=0, scratch=()):
        moved = sum(x.size * x.dtype.itemsize for x in inputs)
        return pl.pallas_call(
            body,
            in_specs=[VMEM] * len(inputs),
            out_specs=[VMEM] * len(outputs),
            out_shape=[jax.ShapeDtypeStruct(*o) for o in outputs],
            scratch_shapes=list(scratch),
            cost_estimate=pl.CostEstimate(flops=flops, bytes_accessed=moved, transcendentals=0),
            compiler_params=pltpu.CompilerParams(vmem_limit_bytes=24 * 2**20),
        )(*inputs)


def stage_body(source, target, arrived):
    copy = pltpu.make_async_copy(source, target, arrived)
    copy.start()
    copy.wait()


def stage(kernel):
    return pl.pallas_call(
        stage_body,
        in_specs=[pl.BlockSpec(memory_space=pl.ANY)],
        out_specs=VMEM,
        out_shape=jax.ShapeDtypeStruct(kernel.shape, kernel.dtype),
        scratch_shapes=[pltpu.SemaphoreType.DMA],
        cost_estimate=pl.CostEstimate(flops=0, bytes_accessed=4 * kernel.size, transcendentals=0),
        compiler_params=pltpu.CompilerParams(vmem_limit_bytes=24 * 2**20),
    )(kernel)


def join_body(own, came, out):
    core = lax.axis_index("img") % 2
    out[pl.ds(core, 1)] = own[...].reshape((1,) + own.shape)
    out[pl.ds(1 - core, 1)] = came[...].reshape((1,) + came.shape)


def join(plan, own):
    return plan.call(join_body, [own, plan.swap(own, 0)], [((2,) + own.shape, own.dtype)])[0]


def place(plan, rows, frame, row_at, lane_at, wide):
    x = rows.astype(F32)
    column = lax.broadcasted_iota(jnp.int32, x.shape, 0) % plan.width
    left = jnp.where(column == 0, 0.0, pltpu.roll(x, 1, 0))
    right = jnp.where(column == plan.width - 1, 0.0, pltpu.roll(x, x.shape[0] - 1, 0))
    for b, moved in enumerate((left, x, right)):
        wide[frame, pl.ds(row_at, x.shape[0]), pl.ds(b * plan.c_in + lane_at, plan.piece)] = moved.astype(BF16)


def clear_edges(plan, wide):
    zero = jnp.zeros((plan.width, wide.shape[2]), BF16)
    for f in range(wide.shape[0]):
        wide[f, 0 : plan.width, :] = zero
        wide[f, plan.width + plan.pixels :, :] = zero


def times(plan, rows, kernel):
    summed = None
    for a in range(3):
        term = jnp.dot(rows(a), kernel[a].reshape(3 * plan.c_in, plan.c_out), preferred_element_type=F32)
        summed = term if summed is None else summed + term
    return summed


def half_rows(plan, wide, core, a):
    blocks = []
    for f in range(wide.shape[0]):
        for pair in range(plan.pairs):
            start = (2 * pair + core) * plan.share + a * plan.width
            blocks.append(wide[f, pl.ds(pl.multiple_of(start, 16), plan.share), :])
    return jnp.concatenate(blocks, axis=0)


def one_sent_body(plan, *refs):
    frames = refs[-1].shape[0]
    pieces, (kernel, *sends, wide) = refs[: frames * plan.ratio], refs[frames * plan.ratio :]
    level, col = where_am_i()
    clear_edges(plan, wide)
    for n, piece in enumerate(pieces):
        place(plan, piece[...], n // plan.ratio, plan.width, plan.lanes(level, n % plan.ratio), wide)
    summed = times(plan, lambda a: half_rows(plan, wide, 1 - col % 2, a), kernel)
    for n, send in enumerate(sends):
        rows = send.shape[0]
        send[...] = summed[n * rows : (n + 1) * rows].astype(BF16)


def one_kept_body(plan, wide, kernel, keep):
    col = lax.axis_index("img")
    keep[...] = times(plan, lambda a: half_rows(plan, wide, col % 2, a), kernel).reshape(keep.shape)


def conv_one_in_two(plan, pieces, kernel, parts):
    frames = len(pieces) // plan.ratio
    half = (frames, plan.pixels // 2, plan.c_out)
    flops = 9 * frames * plan.pixels * plan.c_in * plan.c_out
    outputs = [((half[1] // parts, half[2]), BF16)] * (frames * parts) + [(plan.wide(frames), BF16)]
    *sends, wide = plan.call(functools.partial(one_sent_body, plan), [*pieces, kernel], outputs, flops)
    cames = [plan.swap(send, 0) for send in sends]
    keep = plan.call(functools.partial(one_kept_body, plan), [wide, kernel], [(half, F32)], flops)[0]
    return keep, cames


def halve_body(bit, kept, *refs):
    *cames, keep, send = refs
    frames, half = keep.shape[0], keep.shape[1]
    low = (lax.axis_index("img") // 2**bit) % 2 == 0
    mine = jnp.where(low, 0, half)
    a = pl.ds(pl.multiple_of(mine, 16), half)
    b = pl.ds(pl.multiple_of(half - mine, 16), half)
    for n in range(frames):
        if len(cames) == frames:
            mine_came, other_came = cames[n][a, :], cames[n][b, :]
        else:
            first, second = cames[2 * n][...], cames[2 * n + 1][...]
            mine_came, other_came = jnp.where(low, first, second), jnp.where(low, second, first)
        send[n] = (kept[n, b, :] + other_came.astype(F32)).astype(BF16)
        keep[n] = kept[n, a, :] + mine_came.astype(F32)


def silu_body(kept, came, hidden):
    v = kept[...] + came[...].astype(F32)
    hidden[...] = (v / (1.0 + jnp.exp(-v))).astype(BF16)


def halve(plan, bit, keep, cames):
    half = (keep.shape[0], keep.shape[1] // 2, plan.c_out)
    return plan.call(functools.partial(halve_body, bit), [keep, *cames], [(half, F32), (half, BF16)])


def sum_one(plan, keep, cames):
    keep, send = halve(plan, plan.order[1], keep, cames)
    for n in range(2, plan.bits):
        came = plan.swap(send, plan.order[n - 1])
        keep, send = halve(plan, plan.order[n], keep, [came[f] for f in range(came.shape[0])])
    return keep, send


def add_silu(plan, keep, came):
    return plan.call(silu_body, [keep, came], [(keep.shape, BF16)])[0]


def conv_two_body(plan, chosen, *refs):
    pieces, (kernel, out, wide) = refs[:-3], refs[-3:]
    level, col = where_am_i()
    clear_edges(plan, wide)
    for n, piece in enumerate(pieces):
        turn, e = n // plan.ratio, n % plan.ratio
        pair = (level // plan.ratio + col + turn) % plan.pairs
        for core in range(2):
            row_at = pl.multiple_of(plan.width + (2 * pair + core) * plan.share, 16)
            for f, at in enumerate(chosen):
                place(plan, piece[core, at], f, row_at, plan.lanes(level, e), wide)
    rows = lambda a: wide[:, a * plan.width : a * plan.width + plan.pixels, :].reshape(-1, 3 * plan.c_in)
    out[...] = times(plan, rows, kernel).astype(out.dtype).reshape(out.shape)


def conv_two(plan, pieces, chosen, kernel, dtype):
    frames = len(chosen)
    return plan.call(
        functools.partial(conv_two_body, plan, chosen),
        [*pieces, kernel],
        [((frames, plan.pixels, plan.c_out), dtype)],
        18 * frames * plan.pixels * plan.c_in * plan.c_out,
        [pltpu.VMEM(plan.wide(frames), BF16)],
    )[0]


def conv_for_other(plan, pieces, first, kernel, parts):
    return plan.call(
        functools.partial(for_other_body, plan, first),
        [*pieces, kernel],
        [((plan.pixels // parts, plan.c_out), BF16)] * parts,
        18 * plan.pixels * plan.c_in * plan.c_out,
        [pltpu.VMEM(plan.wide(1), BF16)],
    )


def for_other_body(plan, first, *refs):
    count = plan.pairs * plan.ratio
    pieces, kernel, outs, wide = refs[:count], refs[count], refs[count + 1 : -1], refs[-1]
    level, col = where_am_i()
    clear_edges(plan, wide)
    for n, piece in enumerate(pieces):
        turn, e = n // plan.ratio, n % plan.ratio
        pair = (level // plan.ratio + col + turn) % plan.pairs
        for core in range(2):
            row_at = pl.multiple_of(plan.width + (2 * pair + core) * plan.share, 16)
            place(plan, piece[core, (col + first) % 2], 0, row_at, plan.lanes(level, e), wide)
    total = times(plan, lambda a: wide[0, a * plan.width : a * plan.width + plan.pixels, :], kernel)
    size = plan.pixels // len(outs)
    for n, out in enumerate(outs):
        out[...] = total[n * size : (n + 1) * size].astype(BF16)


def aligned(bit, came, n):
    low = (lax.axis_index("img") // 2**bit) % 2 == 0
    return jnp.where(low, came[n - 1 if n else came.shape[0] - 1].astype(F32), came[n].astype(F32))


def merge_body(bit, at, kept, came, out):
    for n, t in enumerate(at):
        out[n] = (kept[n].astype(F32) + aligned(bit, came, t)).astype(out.dtype)


def merge(plan, bit, kept, came, at, dtype):
    body = functools.partial(merge_body, bit, at)
    return plan.call(body, [kept, came], [(kept.shape, dtype)])[0]


def last_body(kept, first, came, out):
    out[...] = (kept[...] + aligned(0, first, 0)[None] + came[...].astype(F32)).astype(BF16)


def sum_rest(plan, here, first, send):
    if plan.bits == 2:
        came = plan.swap(send, 1)
        return plan.call(last_body, [here, first, came], [(here.shape, BF16)])[0]
    keep = merge(plan, 0, here, first, range(0, 2 * here.shape[0], 2), F32)
    for bit in range(1, plan.bits):
        came = plan.swap(send, bit)
        count = keep.shape[0]
        total = merge(plan, bit, keep, came, range(count), F32 if count > 1 else BF16)
        keep, send = total[0::2], total[1::2].astype(BF16)
    return total


def part_of(plan, part):
    level, col = where_am_i()
    first = (level // plan.ratio + col) % plan.pairs == 0
    size = plan.pixels // 2 - plan.width
    if part == 0:
        return jnp.where(first, 0, plan.pixels - size), size
    if part == 1:
        return jnp.where(first, size, 0), plan.pixels - size
    return 0, plan.pixels


def part_body(plan, part, frame, turns, *refs):
    count = turns * plan.ratio
    pieces, kernel, cames, (out, wide, added) = refs[:count], refs[count], refs[count + 1 : -3], refs[-3:]
    level, col = where_am_i()
    clear_edges(plan, wide)
    for n, piece in enumerate(pieces):
        turn, e = n // plan.ratio, n % plan.ratio
        pair = (level // plan.ratio + col + turn) % plan.pairs
        for core in range(2):
            row_at = pl.multiple_of(plan.width + (2 * pair + core) * plan.share, 16)
            place(plan, piece[core, frame], 0, row_at, plan.lanes(level, e), wide)
    for n, came in enumerate(cames):
        added[n * came.shape[0] : (n + 1) * came.shape[0], :] = came[...]
    start, size = part_of(plan, part)
    at = lambda a: pl.ds(pl.multiple_of(start + a * plan.width, 16), size)
    total = times(plan, lambda a: wide[0, at(a), :], kernel)
    out[...] = (total + added[at(0), :].astype(F32)).astype(out.dtype)


def conv_part(plan, part, frame, pieces, kernel, cames, dtype):
    size = [plan.pixels // 2 - plan.width, plan.pixels // 2 + plan.width, plan.pixels][part]
    return plan.call(
        functools.partial(part_body, plan, part, frame, len(pieces) // plan.ratio),
        [*pieces, kernel, *cames],
        [((size, plan.c_out), dtype)],
        18 * size * plan.c_in * plan.c_out,
        [pltpu.VMEM(plan.wide(1), BF16), pltpu.VMEM((plan.pixels, plan.c_out), BF16)],
    )[0]


def put_body(plan, kept, *refs):
    *cames, out = refs
    for part, came in enumerate(cames):
        start, size = part_of(plan, part)
        rows = pl.ds(pl.multiple_of(start, 16), size)
        out[rows, :] = (kept[rows, :] + came[...].astype(F32)).astype(BF16)


def sum_in_parts(plan, odds, evens, hidden, kernel):
    odds = after(odds, hidden)
    frames = len(odds[0][0])
    if plan.pairs != 2:
        sums = conv_two(plan, odds, range(frames), kernel, BF16)
        came = plan.swap(after(sums, evens), 0)
        here = conv_two(plan, evens, range(frames // 2), kernel, F32)
        send = merge(plan, 0, here, came, range(1, frames, 2), BF16)
        here = conv_two(plan, evens, range(frames // 2, frames), kernel, F32)
        return sum_rest(plan, here, came, send)
    cames = [plan.swap(part, 0) for part in conv_for_other(plan, odds, 1, kernel, 2)]
    own = conv_for_other(plan, odds, 0, kernel, 1)[0]
    near, both = after(evens[: plan.ratio], own), evens
    sums = conv_part(plan, 0, 0, near, kernel, cames, BF16)
    early = plan.swap(sums, 1)
    sums = conv_part(plan, 1, 0, after(both, sums), kernel, cames, BF16)
    late = plan.swap(sums, 1)
    early = after(early, sums)
    kept = conv_part(plan, 2, 1, after(both, early), kernel, [plan.swap(own, 0)], F32)
    body = functools.partial(put_body, plan)
    return plan.call(body, [kept, early, late], [(kept.shape, BF16)])[0]


def shards(mesh, features, kernel_one, kernel_two):
    plan = Plan(mesh, features, kernel_one)
    block = features.reshape(plan.pixels, plan.piece)
    odd = list(range(1, plan.cols, 2))
    even = list(range(2, plan.cols, 4)) + list(range(0, plan.cols, 4))
    early = [p for d in odd for p in plan.spread_frame(block, d)]
    kernel_one = stage(kernel_one)
    late = [p for d in even for p in plan.spread_frame(block, d)]
    last = plan.order[-1]
    keep, ahead = sum_one(plan, *conv_one_in_two(plan, early, kernel_one, 1))
    kept, cames = conv_one_in_two(plan, after(late, ahead), kernel_one, 2)
    kept, behind = sum_one(plan, kept, cames)
    hidden = join(plan, add_silu(plan, keep, after(plan.swap(ahead, last), behind)))
    odds = [p for t in range(plan.pairs) for p in plan.spread(hidden, t)]
    hidden = join(plan, add_silu(plan, kept, plan.swap(behind, last)))
    evens = [p for t in range(plan.pairs) for p in plan.spread(hidden, t)]
    return sum_in_parts(plan, odds, evens, hidden, kernel_two).reshape(features.shape)


def solution(mesh):
    placed = (
        P(("groups", "img"), None, None, "chan"),
        P(None, None, "img", "chan"),
        P(None, None, "img", "chan"),
    )
    return jax.shard_map(
        functools.partial(shards, mesh),
        mesh=mesh,
        in_specs=placed,
        out_specs=P(("groups", "img"), None, None, "chan"),
        check_vma=False,
    )
```

```python
import functools

import jax
import jax.numpy as jnp
from jax import lax
from jax.experimental import pallas as pl
from jax.experimental.pallas import tpu as pltpu
from jax.sharding import PartitionSpec as P

VMEM = pl.BlockSpec(memory_space=pltpu.VMEM)
F32, BF16 = jnp.float32, jnp.bfloat16


def where_am_i():
    return lax.axis_index("chan"), lax.axis_index("img")


def after(x, *first):
    return lax.optimization_barrier((x, first))[0]


class Plan:
    def __init__(self, mesh, features, kernel):
        self.levels, self.cols = mesh.shape["chan"], mesh.shape["img"]
        self.pairs, self.ratio = self.cols // 2, self.levels // self.cols
        self.width = features.shape[2]
        self.pixels = features.shape[1] * features.shape[2]
        self.piece = features.shape[3]
        self.c_in, self.c_out = kernel.shape[2], kernel.shape[3]
        self.share = self.pixels // self.cols
        self.bits = self.cols.bit_length() - 1
        self.order = [0, *range(self.bits - 1, 0, -1)]

    def wide(self, frames):
        return (frames, self.pixels + 2 * self.width, 3 * self.c_in)

    def spread_frame(self, x, turn):
        taken = []
        for e in range(self.ratio):
            moves = []
            for k in range(self.levels):
                for f in range(self.cols):
                    level = (f - turn) % self.cols * self.ratio + (k % self.ratio - e) % self.ratio
                    moves.append((k * self.cols + f, level * self.cols + k // self.ratio))
            taken.append(lax.ppermute(x, ("chan", "img"), moves))
        return taken

    def pair_of(self, half, level, col, turn):
        return (level // self.ratio + turn + (col if half else 1)) % self.pairs

    def spread(self, x, half, turn):
        taken = []
        for e in range(self.ratio):
            moves = []
            for level in range(self.levels):
                v, u = level // self.ratio, level % self.ratio
                core = v // self.pairs
                for col in range(self.cols):
                    pair = self.pair_of(half, level, col, turn)
                    source = col * self.ratio + (u + e) % self.ratio
                    moves.append((source * self.cols + 2 * pair + core, level * self.cols + col))
            taken.append(lax.ppermute(x, ("chan", "img"), moves))
        return taken

    def lanes(self, level, e):
        if self.ratio == 1:
            return 0
        return pl.multiple_of((level + e) % self.ratio * self.piece, 128)

    def swap(self, x, bit):
        return lax.ppermute(x, "img", [(i, i ^ (1 << bit)) for i in range(self.cols)])

    def call(self, body, inputs, outputs, flops=0, scratch=()):
        moved = sum(x.size * x.dtype.itemsize for x in inputs)
        return pl.pallas_call(
            body,
            in_specs=[VMEM] * len(inputs),
            out_specs=[VMEM] * len(outputs),
            out_shape=[jax.ShapeDtypeStruct(*o) for o in outputs],
            scratch_shapes=list(scratch),
            cost_estimate=pl.CostEstimate(flops=flops, bytes_accessed=moved, transcendentals=0),
            compiler_params=pltpu.CompilerParams(vmem_limit_bytes=24 * 2**20),
        )(*inputs)


def stage_body(source, target, arrived):
    copy = pltpu.make_async_copy(source, target, arrived)
    copy.start()
    copy.wait()


def stage(kernel):
    return pl.pallas_call(
        stage_body,
        in_specs=[pl.BlockSpec(memory_space=pl.ANY)],
        out_specs=VMEM,
        out_shape=jax.ShapeDtypeStruct(kernel.shape, kernel.dtype),
        scratch_shapes=[pltpu.SemaphoreType.DMA],
        cost_estimate=pl.CostEstimate(flops=0, bytes_accessed=4 * kernel.size, transcendentals=0),
        compiler_params=pltpu.CompilerParams(vmem_limit_bytes=24 * 2**20),
    )(kernel)


def join_body(own, came, out):
    core = lax.axis_index("img") % 2
    out[pl.ds(core, 1)] = own[...].reshape((1,) + own.shape)
    out[pl.ds(1 - core, 1)] = came[...].reshape((1,) + came.shape)


def join(plan, own):
    return plan.call(join_body, [own, plan.swap(own, 0)], [((2,) + own.shape, own.dtype)])[0]


def place(plan, rows, frame, row_at, lane_at, wide):
    x = rows.astype(F32)
    column = lax.broadcasted_iota(jnp.int32, x.shape, 0) % plan.width
    left = jnp.where(column == 0, 0.0, pltpu.roll(x, 1, 0))
    right = jnp.where(column == plan.width - 1, 0.0, pltpu.roll(x, x.shape[0] - 1, 0))
    for b, moved in enumerate((left, x, right)):
        wide[frame, pl.ds(row_at, x.shape[0]), pl.ds(b * plan.c_in + lane_at, plan.piece)] = moved.astype(BF16)


def clear_edges(plan, wide):
    zero = jnp.zeros((plan.width, wide.shape[2]), BF16)
    for f in range(wide.shape[0]):
        wide[f, 0 : plan.width, :] = zero
        wide[f, plan.width + plan.pixels :, :] = zero


def times(plan, rows, kernel):
    summed = None
    for a in range(3):
        term = jnp.dot(rows(a), kernel[a].reshape(3 * plan.c_in, plan.c_out), preferred_element_type=F32)
        summed = term if summed is None else summed + term
    return summed


def half_rows(plan, wide, core, a):
    blocks = []
    for f in range(wide.shape[0]):
        for pair in range(plan.pairs):
            start = (2 * pair + core) * plan.share + a * plan.width
            blocks.append(wide[f, pl.ds(pl.multiple_of(start, 16), plan.share), :])
    return jnp.concatenate(blocks, axis=0)


def one_sent_body(plan, *refs):
    frames = refs[-1].shape[0]
    pieces, (kernel, *sends, wide) = refs[: frames * plan.ratio], refs[frames * plan.ratio :]
    level, col = where_am_i()
    clear_edges(plan, wide)
    for n, piece in enumerate(pieces):
        place(plan, piece[...], n // plan.ratio, plan.width, plan.lanes(level, n % plan.ratio), wide)
    summed = times(plan, lambda a: half_rows(plan, wide, 1 - col % 2, a), kernel)
    for n, send in enumerate(sends):
        rows = send.shape[0]
        send[...] = summed[n * rows : (n + 1) * rows].astype(BF16)


def one_kept_body(plan, wide, kernel, keep):
    col = lax.axis_index("img")
    keep[...] = times(plan, lambda a: half_rows(plan, wide, col % 2, a), kernel).reshape(keep.shape)


def conv_one_in_two(plan, pieces, kernel, parts):
    frames = len(pieces) // plan.ratio
    half = (frames, plan.pixels // 2, plan.c_out)
    flops = 9 * frames * plan.pixels * plan.c_in * plan.c_out
    outputs = [((half[1] // parts, half[2]), BF16)] * (frames * parts) + [(plan.wide(frames), BF16)]
    *sends, wide = plan.call(functools.partial(one_sent_body, plan), [*pieces, kernel], outputs, flops)
    cames = [plan.swap(send, 0) for send in sends]
    keep = plan.call(functools.partial(one_kept_body, plan), [wide, kernel], [(half, F32)], flops)[0]
    return keep, cames


def halve_body(bit, kept, *refs):
    *cames, keep, send = refs
    frames, half = keep.shape[0], keep.shape[1]
    low = (lax.axis_index("img") // 2**bit) % 2 == 0
    mine = jnp.where(low, 0, half)
    a = pl.ds(pl.multiple_of(mine, 16), half)
    b = pl.ds(pl.multiple_of(half - mine, 16), half)
    for n in range(frames):
        if len(cames) == frames:
            mine_came, other_came = cames[n][a, :], cames[n][b, :]
        else:
            first, second = cames[2 * n][...], cames[2 * n + 1][...]
            mine_came, other_came = jnp.where(low, first, second), jnp.where(low, second, first)
        send[n] = (kept[n, b, :] + other_came.astype(F32)).astype(BF16)
        keep[n] = kept[n, a, :] + mine_came.astype(F32)


def silu_body(kept, came, hidden):
    v = kept[...] + came[...].astype(F32)
    hidden[...] = (v / (1.0 + jnp.exp(-v))).astype(BF16)


def halve(plan, bit, keep, cames):
    half = (keep.shape[0], keep.shape[1] // 2, plan.c_out)
    return plan.call(functools.partial(halve_body, bit), [keep, *cames], [(half, F32), (half, BF16)])


def sum_one(plan, keep, cames):
    keep, send = halve(plan, plan.order[1], keep, cames)
    for n in range(2, plan.bits):
        came = plan.swap(send, plan.order[n - 1])
        keep, send = halve(plan, plan.order[n], keep, [came[f] for f in range(came.shape[0])])
    return keep, send


def add_silu(plan, keep, came):
    return plan.call(silu_body, [keep, came], [(keep.shape, BF16)])[0]


def conv_two_body(plan, half, chosen, *refs):
    pieces, (kernel, out, wide) = refs[:-3], refs[-3:]
    level, col = where_am_i()
    clear_edges(plan, wide)
    for n, piece in enumerate(pieces):
        turn, e = n // plan.ratio, n % plan.ratio
        pair = plan.pair_of(half, level, col, turn)
        for core in range(2):
            row_at = pl.multiple_of(plan.width + (2 * pair + core) * plan.share, 16)
            for f, at in enumerate(chosen):
                place(plan, piece[core, at], f, row_at, plan.lanes(level, e), wide)
    rows = lambda a: wide[:, a * plan.width : a * plan.width + plan.pixels, :].reshape(-1, 3 * plan.c_in)
    out[...] = times(plan, rows, kernel).astype(out.dtype).reshape(out.shape)


def conv_two(plan, half, pieces, chosen, kernel, dtype):
    frames = len(chosen)
    return plan.call(
        functools.partial(conv_two_body, plan, half, chosen),
        [*pieces, kernel],
        [((frames, plan.pixels, plan.c_out), dtype)],
        18 * frames * plan.pixels * plan.c_in * plan.c_out,
        [pltpu.VMEM(plan.wide(frames), BF16)],
    )[0]


def conv_for_other(plan, pieces, first, kernel, parts):
    return plan.call(
        functools.partial(for_other_body, plan, first),
        [*pieces, kernel],
        [((plan.pixels // parts, plan.c_out), BF16)] * parts,
        18 * plan.pixels * plan.c_in * plan.c_out,
        [pltpu.VMEM(plan.wide(1), BF16)],
    )


def for_other_body(plan, first, *refs):
    count = plan.pairs * plan.ratio
    pieces, kernel, outs, wide = refs[:count], refs[count], refs[count + 1 : -1], refs[-1]
    level, col = where_am_i()
    clear_edges(plan, wide)
    for n, piece in enumerate(pieces):
        turn, e = n // plan.ratio, n % plan.ratio
        pair = plan.pair_of(0, level, col, turn)
        for core in range(2):
            row_at = pl.multiple_of(plan.width + (2 * pair + core) * plan.share, 16)
            place(plan, piece[core, (col + first) % 2], 0, row_at, plan.lanes(level, e), wide)
    total = times(plan, lambda a: wide[0, a * plan.width : a * plan.width + plan.pixels, :], kernel)
    size = plan.pixels // len(outs)
    for n, out in enumerate(outs):
        out[...] = total[n * size : (n + 1) * size].astype(BF16)


def aligned(bit, came, n):
    low = (lax.axis_index("img") // 2**bit) % 2 == 0
    return jnp.where(low, came[n - 1 if n else came.shape[0] - 1].astype(F32), came[n].astype(F32))


def merge_body(bit, at, kept, came, out):
    for n, t in enumerate(at):
        out[n] = (kept[n].astype(F32) + aligned(bit, came, t)).astype(out.dtype)


def merge(plan, bit, kept, came, at, dtype):
    body = functools.partial(merge_body, bit, at)
    return plan.call(body, [kept, came], [(kept.shape, dtype)])[0]


def last_body(kept, first, came, out):
    out[...] = (kept[...] + aligned(0, first, 0)[None] + came[...].astype(F32)).astype(BF16)


def sum_rest(plan, here, first, send):
    if plan.bits == 2:
        came = plan.swap(send, 1)
        return plan.call(last_body, [here, first, came], [(here.shape, BF16)])[0]
    keep = merge(plan, 0, here, first, range(0, 2 * here.shape[0], 2), F32)
    for bit in range(1, plan.bits):
        came = plan.swap(send, bit)
        count = keep.shape[0]
        total = merge(plan, bit, keep, came, range(count), F32 if count > 1 else BF16)
        keep, send = total[0::2], total[1::2].astype(BF16)
    return total


def part_of(plan, part):
    level, col = where_am_i()
    first = plan.pair_of(1, level, col, 0) == 0
    size = plan.pixels // 2 - plan.width
    if part == 0:
        return jnp.where(first, 0, plan.pixels - size), size
    if part == 1:
        return jnp.where(first, size, 0), plan.pixels - size
    return 0, plan.pixels


def part_body(plan, part, frame, turns, *refs):
    count = turns * plan.ratio
    pieces, kernel, cames, (out, wide, added) = refs[:count], refs[count], refs[count + 1 : -3], refs[-3:]
    level, col = where_am_i()
    clear_edges(plan, wide)
    for n, piece in enumerate(pieces):
        turn, e = n // plan.ratio, n % plan.ratio
        pair = plan.pair_of(1, level, col, turn)
        for core in range(2):
            row_at = pl.multiple_of(plan.width + (2 * pair + core) * plan.share, 16)
            place(plan, piece[core, frame], 0, row_at, plan.lanes(level, e), wide)
    for n, came in enumerate(cames):
        added[n * came.shape[0] : (n + 1) * came.shape[0], :] = came[...]
    start, size = part_of(plan, part)
    at = lambda a: pl.ds(pl.multiple_of(start + a * plan.width, 16), size)
    total = times(plan, lambda a: wide[0, at(a), :], kernel)
    out[...] = (total + added[at(0), :].astype(F32)).astype(out.dtype)


def conv_part(plan, part, frame, pieces, kernel, cames, dtype):
    size = [plan.pixels // 2 - plan.width, plan.pixels // 2 + plan.width, plan.pixels][part]
    return plan.call(
        functools.partial(part_body, plan, part, frame, len(pieces) // plan.ratio),
        [*pieces, kernel, *cames],
        [((size, plan.c_out), dtype)],
        18 * size * plan.c_in * plan.c_out,
        [pltpu.VMEM(plan.wide(1), BF16), pltpu.VMEM((plan.pixels, plan.c_out), BF16)],
    )[0]


def put_body(plan, kept, *refs):
    *cames, out = refs
    for part, came in enumerate(cames):
        start, size = part_of(plan, part)
        rows = pl.ds(pl.multiple_of(start, 16), size)
        out[rows, :] = (kept[rows, :] + came[...].astype(F32)).astype(BF16)


def sum_in_parts(plan, odds, evens, hidden, kernel):
    odds = after(odds, hidden)
    frames = len(odds[0][0])
    if plan.pairs != 2:
        sums = conv_two(plan, 0, odds, range(frames), kernel, BF16)
        came = plan.swap(after(sums, evens), 0)
        here = conv_two(plan, 1, evens, range(frames // 2), kernel, F32)
        send = merge(plan, 0, here, came, range(1, frames, 2), BF16)
        here = conv_two(plan, 1, evens, range(frames // 2, frames), kernel, F32)
        return sum_rest(plan, here, came, send)
    cames = [plan.swap(part, 0) for part in conv_for_other(plan, odds, 1, kernel, 2)]
    own = conv_for_other(plan, odds, 0, kernel, 1)[0]
    near, both = after(evens[: plan.ratio], own), evens
    sums = conv_part(plan, 0, 0, near, kernel, cames, BF16)
    early = plan.swap(sums, 1)
    sums = conv_part(plan, 1, 0, after(both, sums), kernel, cames, BF16)
    late = plan.swap(sums, 1)
    early = after(early, sums)
    kept = conv_part(plan, 2, 1, after(both, early), kernel, [plan.swap(own, 0)], F32)
    body = functools.partial(put_body, plan)
    return plan.call(body, [kept, early, late], [(kept.shape, BF16)])[0]


def shards(mesh, features, kernel_one, kernel_two):
    plan = Plan(mesh, features, kernel_one)
    block = features.reshape(plan.pixels, plan.piece)
    odd = list(range(1, plan.cols, 2))
    even = list(range(2, plan.cols, 4)) + list(range(0, plan.cols, 4))
    early = [p for d in odd for p in plan.spread_frame(block, d)]
    kernel_one = stage(kernel_one)
    late = [p for d in even for p in plan.spread_frame(block, d)]
    last = plan.order[-1]
    keep, ahead = sum_one(plan, *conv_one_in_two(plan, early, kernel_one, 1))
    kept, cames = conv_one_in_two(plan, after(late, ahead), kernel_one, 2)
    kept, behind = sum_one(plan, kept, cames)
    hidden = join(plan, add_silu(plan, keep, after(plan.swap(ahead, last), behind)))
    odds = [p for t in range(plan.pairs) for p in plan.spread(hidden, 0, t)]
    hidden = join(plan, add_silu(plan, kept, plan.swap(behind, last)))
    evens = [p for t in range(plan.pairs) for p in plan.spread(hidden, 1, t)]
    return sum_in_parts(plan, odds, evens, hidden, kernel_two).reshape(features.shape)


def solution(mesh):
    placed = (
        P(("groups", "img"), None, None, "chan"),
        P(None, None, "img", "chan"),
        P(None, None, "img", "chan"),
    )
    return jax.shard_map(
        functools.partial(shards, mesh),
        mesh=mesh,
        in_specs=placed,
        out_specs=P(("groups", "img"), None, None, "chan"),
        check_vma=False,
    )
```

```python
import functools

import jax
import jax.numpy as jnp
from jax import lax
from jax.experimental import pallas as pl
from jax.experimental.pallas import tpu as pltpu
from jax.sharding import PartitionSpec as P

VMEM = pl.BlockSpec(memory_space=pltpu.VMEM)
F32, BF16 = jnp.float32, jnp.bfloat16


def where_am_i():
    return lax.axis_index("chan"), lax.axis_index("img")


def after(x, *first):
    return lax.optimization_barrier((x, first))[0]


class Plan:
    def __init__(self, mesh, features, kernel):
        self.levels, self.cols = mesh.shape["chan"], mesh.shape["img"]
        self.pairs, self.ratio = self.cols // 2, self.levels // self.cols
        self.width = features.shape[2]
        self.pixels = features.shape[1] * features.shape[2]
        self.piece = features.shape[3]
        self.c_in, self.c_out = kernel.shape[2], kernel.shape[3]
        self.share = self.pixels // self.cols
        self.bits = self.cols.bit_length() - 1
        self.order = [0, *range(self.bits - 1, 0, -1)]

    def wide(self, frames):
        return (frames, self.pixels + 2 * self.width, 3 * self.c_in)

    def spread_frame(self, x, turn):
        taken = []
        for e in range(self.ratio):
            moves = []
            for k in range(self.levels):
                for f in range(self.cols):
                    level = (f - turn) % self.cols * self.ratio + (k % self.ratio - e) % self.ratio
                    moves.append((k * self.cols + f, level * self.cols + k // self.ratio))
            taken.append(lax.ppermute(x, ("chan", "img"), moves))
        return taken

    def pair_of(self, half, level, col, turn):
        return (level // self.ratio + turn + 1 + (col if half else 0)) % self.pairs

    def spread(self, x, half, turn):
        taken = []
        for e in range(self.ratio):
            moves = []
            for level in range(self.levels):
                v, u = level // self.ratio, level % self.ratio
                core = v // self.pairs
                for col in range(self.cols):
                    pair = self.pair_of(half, level, col, turn)
                    source = col * self.ratio + (u + e) % self.ratio
                    moves.append((source * self.cols + 2 * pair + core, level * self.cols + col))
            taken.append(lax.ppermute(x, ("chan", "img"), moves))
        return taken

    def lanes(self, level, e):
        if self.ratio == 1:
            return 0
        return pl.multiple_of((level + e) % self.ratio * self.piece, 128)

    def swap(self, x, bit):
        return lax.ppermute(x, "img", [(i, i ^ (1 << bit)) for i in range(self.cols)])

    def call(self, body, inputs, outputs, flops=0, scratch=()):
        moved = sum(x.size * x.dtype.itemsize for x in inputs)
        return pl.pallas_call(
            body,
            in_specs=[VMEM] * len(inputs),
            out_specs=[VMEM] * len(outputs),
            out_shape=[jax.ShapeDtypeStruct(*o) for o in outputs],
            scratch_shapes=list(scratch),
            cost_estimate=pl.CostEstimate(flops=flops, bytes_accessed=moved, transcendentals=0),
            compiler_params=pltpu.CompilerParams(vmem_limit_bytes=24 * 2**20),
        )(*inputs)


def stage_body(source, target, arrived):
    copy = pltpu.make_async_copy(source, target, arrived)
    copy.start()
    copy.wait()


def stage(kernel):
    return pl.pallas_call(
        stage_body,
        in_specs=[pl.BlockSpec(memory_space=pl.ANY)],
        out_specs=VMEM,
        out_shape=jax.ShapeDtypeStruct(kernel.shape, kernel.dtype),
        scratch_shapes=[pltpu.SemaphoreType.DMA],
        cost_estimate=pl.CostEstimate(flops=0, bytes_accessed=4 * kernel.size, transcendentals=0),
        compiler_params=pltpu.CompilerParams(vmem_limit_bytes=24 * 2**20),
    )(kernel)


def join_body(own, came, out):
    core = lax.axis_index("img") % 2
    out[pl.ds(core, 1)] = own[...].reshape((1,) + own.shape)
    out[pl.ds(1 - core, 1)] = came[...].reshape((1,) + came.shape)


def join(plan, own):
    return plan.call(join_body, [own, plan.swap(own, 0)], [((2,) + own.shape, own.dtype)])[0]


def place(plan, rows, frame, row_at, lane_at, wide):
    x = rows.astype(F32)
    column = lax.broadcasted_iota(jnp.int32, x.shape, 0) % plan.width
    left = jnp.where(column == 0, 0.0, pltpu.roll(x, 1, 0))
    right = jnp.where(column == plan.width - 1, 0.0, pltpu.roll(x, x.shape[0] - 1, 0))
    for b, moved in enumerate((left, x, right)):
        wide[frame, pl.ds(row_at, x.shape[0]), pl.ds(b * plan.c_in + lane_at, plan.piece)] = moved.astype(BF16)


def clear_edges(plan, wide):
    zero = jnp.zeros((plan.width, wide.shape[2]), BF16)
    for f in range(wide.shape[0]):
        wide[f, 0 : plan.width, :] = zero
        wide[f, plan.width + plan.pixels :, :] = zero


def times(plan, rows, kernel):
    summed = None
    for a in range(3):
        term = jnp.dot(rows(a), kernel[a].reshape(3 * plan.c_in, plan.c_out), preferred_element_type=F32)
        summed = term if summed is None else summed + term
    return summed


def half_rows(plan, wide, core, a):
    blocks = []
    for f in range(wide.shape[0]):
        for pair in range(plan.pairs):
            start = (2 * pair + core) * plan.share + a * plan.width
            blocks.append(wide[f, pl.ds(pl.multiple_of(start, 16), plan.share), :])
    return jnp.concatenate(blocks, axis=0)


def one_sent_body(plan, *refs):
    frames = refs[-1].shape[0]
    pieces, (kernel, *sends, wide) = refs[: frames * plan.ratio], refs[frames * plan.ratio :]
    level, col = where_am_i()
    clear_edges(plan, wide)
    for n, piece in enumerate(pieces):
        place(plan, piece[...], n // plan.ratio, plan.width, plan.lanes(level, n % plan.ratio), wide)
    summed = times(plan, lambda a: half_rows(plan, wide, 1 - col % 2, a), kernel)
    for n, send in enumerate(sends):
        rows = send.shape[0]
        send[...] = summed[n * rows : (n + 1) * rows].astype(BF16)


def one_kept_body(plan, wide, kernel, keep):
    col = lax.axis_index("img")
    keep[...] = times(plan, lambda a: half_rows(plan, wide, col % 2, a), kernel).reshape(keep.shape)


def conv_one_in_two(plan, pieces, kernel, parts):
    frames = len(pieces) // plan.ratio
    half = (frames, plan.pixels // 2, plan.c_out)
    flops = 9 * frames * plan.pixels * plan.c_in * plan.c_out
    outputs = [((half[1] // parts, half[2]), BF16)] * (frames * parts) + [(plan.wide(frames), BF16)]
    *sends, wide = plan.call(functools.partial(one_sent_body, plan), [*pieces, kernel], outputs, flops)
    cames = [plan.swap(send, 0) for send in sends]
    keep = plan.call(functools.partial(one_kept_body, plan), [wide, kernel], [(half, F32)], flops)[0]
    return keep, cames


def halve_body(bit, kept, *refs):
    *cames, keep, send = refs
    frames, half = keep.shape[0], keep.shape[1]
    low = (lax.axis_index("img") // 2**bit) % 2 == 0
    mine = jnp.where(low, 0, half)
    a = pl.ds(pl.multiple_of(mine, 16), half)
    b = pl.ds(pl.multiple_of(half - mine, 16), half)
    for n in range(frames):
        if len(cames) == frames:
            mine_came, other_came = cames[n][a, :], cames[n][b, :]
        else:
            first, second = cames[2 * n][...], cames[2 * n + 1][...]
            mine_came, other_came = jnp.where(low, first, second), jnp.where(low, second, first)
        send[n] = (kept[n, b, :] + other_came.astype(F32)).astype(BF16)
        keep[n] = kept[n, a, :] + mine_came.astype(F32)


def silu_body(kept, came, hidden):
    v = kept[...] + came[...].astype(F32)
    hidden[...] = (v / (1.0 + jnp.exp(-v))).astype(BF16)


def halve(plan, bit, keep, cames):
    half = (keep.shape[0], keep.shape[1] // 2, plan.c_out)
    return plan.call(functools.partial(halve_body, bit), [keep, *cames], [(half, F32), (half, BF16)])


def sum_one(plan, keep, cames):
    keep, send = halve(plan, plan.order[1], keep, cames)
    for n in range(2, plan.bits):
        came = plan.swap(send, plan.order[n - 1])
        keep, send = halve(plan, plan.order[n], keep, [came[f] for f in range(came.shape[0])])
    return keep, send


def add_silu(plan, keep, came):
    return plan.call(silu_body, [keep, came], [(keep.shape, BF16)])[0]


def conv_two_body(plan, half, chosen, *refs):
    pieces, (kernel, out, wide) = refs[:-3], refs[-3:]
    level, col = where_am_i()
    clear_edges(plan, wide)
    for n, piece in enumerate(pieces):
        turn, e = n // plan.ratio, n % plan.ratio
        pair = plan.pair_of(half, level, col, turn)
        for core in range(2):
            row_at = pl.multiple_of(plan.width + (2 * pair + core) * plan.share, 16)
            for f, at in enumerate(chosen):
                place(plan, piece[core, at], f, row_at, plan.lanes(level, e), wide)
    rows = lambda a: wide[:, a * plan.width : a * plan.width + plan.pixels, :].reshape(-1, 3 * plan.c_in)
    out[...] = times(plan, rows, kernel).astype(out.dtype).reshape(out.shape)


def conv_two(plan, half, pieces, chosen, kernel, dtype):
    frames = len(chosen)
    return plan.call(
        functools.partial(conv_two_body, plan, half, chosen),
        [*pieces, kernel],
        [((frames, plan.pixels, plan.c_out), dtype)],
        18 * frames * plan.pixels * plan.c_in * plan.c_out,
        [pltpu.VMEM(plan.wide(frames), BF16)],
    )[0]


def conv_for_other(plan, pieces, first, kernel, parts):
    return plan.call(
        functools.partial(for_other_body, plan, first),
        [*pieces, kernel],
        [((plan.pixels // parts, plan.c_out), BF16)] * parts,
        18 * plan.pixels * plan.c_in * plan.c_out,
        [pltpu.VMEM(plan.wide(1), BF16)],
    )


def for_other_body(plan, first, *refs):
    count = plan.pairs * plan.ratio
    pieces, kernel, outs, wide = refs[:count], refs[count], refs[count + 1 : -1], refs[-1]
    level, col = where_am_i()
    clear_edges(plan, wide)
    for n, piece in enumerate(pieces):
        turn, e = n // plan.ratio, n % plan.ratio
        pair = plan.pair_of(0, level, col, turn)
        for core in range(2):
            row_at = pl.multiple_of(plan.width + (2 * pair + core) * plan.share, 16)
            place(plan, piece[core, (col + first) % 2], 0, row_at, plan.lanes(level, e), wide)
    total = times(plan, lambda a: wide[0, a * plan.width : a * plan.width + plan.pixels, :], kernel)
    size = plan.pixels // len(outs)
    for n, out in enumerate(outs):
        out[...] = total[n * size : (n + 1) * size].astype(BF16)


def aligned(bit, came, n):
    low = (lax.axis_index("img") // 2**bit) % 2 == 0
    return jnp.where(low, came[n - 1 if n else came.shape[0] - 1].astype(F32), came[n].astype(F32))


def merge_body(bit, at, kept, came, out):
    for n, t in enumerate(at):
        out[n] = (kept[n].astype(F32) + aligned(bit, came, t)).astype(out.dtype)


def merge(plan, bit, kept, came, at, dtype):
    body = functools.partial(merge_body, bit, at)
    return plan.call(body, [kept, came], [(kept.shape, dtype)])[0]


def last_body(kept, first, came, out):
    out[...] = (kept[...] + aligned(0, first, 0)[None] + came[...].astype(F32)).astype(BF16)


def sum_rest(plan, here, first, send):
    if plan.bits == 2:
        came = plan.swap(send, 1)
        return plan.call(last_body, [here, first, came], [(here.shape, BF16)])[0]
    keep = merge(plan, 0, here, first, range(0, 2 * here.shape[0], 2), F32)
    for bit in range(1, plan.bits):
        came = plan.swap(send, bit)
        count = keep.shape[0]
        total = merge(plan, bit, keep, came, range(count), F32 if count > 1 else BF16)
        keep, send = total[0::2], total[1::2].astype(BF16)
    return total


def part_of(plan, part):
    level, col = where_am_i()
    first = plan.pair_of(1, level, col, 0) == 0
    size = plan.pixels // 2 - plan.width
    if part == 0:
        return jnp.where(first, 0, plan.pixels - size), size
    if part == 1:
        return jnp.where(first, size, 0), plan.pixels - size
    return 0, plan.pixels


def part_body(plan, part, frame, turns, *refs):
    count = turns * plan.ratio
    pieces, kernel, cames, (out, wide, added) = refs[:count], refs[count], refs[count + 1 : -3], refs[-3:]
    level, col = where_am_i()
    clear_edges(plan, wide)
    for n, piece in enumerate(pieces):
        turn, e = n // plan.ratio, n % plan.ratio
        pair = plan.pair_of(1, level, col, turn)
        for core in range(2):
            row_at = pl.multiple_of(plan.width + (2 * pair + core) * plan.share, 16)
            place(plan, piece[core, frame], 0, row_at, plan.lanes(level, e), wide)
    for n, came in enumerate(cames):
        added[n * came.shape[0] : (n + 1) * came.shape[0], :] = came[...]
    start, size = part_of(plan, part)
    at = lambda a: pl.ds(pl.multiple_of(start + a * plan.width, 16), size)
    total = times(plan, lambda a: wide[0, at(a), :], kernel)
    out[...] = (total + added[at(0), :].astype(F32)).astype(out.dtype)


def conv_part(plan, part, frame, pieces, kernel, cames, dtype):
    size = [plan.pixels // 2 - plan.width, plan.pixels // 2 + plan.width, plan.pixels][part]
    return plan.call(
        functools.partial(part_body, plan, part, frame, len(pieces) // plan.ratio),
        [*pieces, kernel, *cames],
        [((size, plan.c_out), dtype)],
        18 * size * plan.c_in * plan.c_out,
        [pltpu.VMEM(plan.wide(1), BF16), pltpu.VMEM((plan.pixels, plan.c_out), BF16)],
    )[0]


def put_body(plan, kept, *refs):
    *cames, out = refs
    for part, came in enumerate(cames):
        start, size = part_of(plan, part)
        rows = pl.ds(pl.multiple_of(start, 16), size)
        out[rows, :] = (kept[rows, :] + came[...].astype(F32)).astype(BF16)


def sum_in_parts(plan, odds, evens, hidden, kernel):
    odds = after(odds, hidden)
    frames = len(odds[0][0])
    if plan.pairs != 2:
        sums = conv_two(plan, 0, odds, range(frames), kernel, BF16)
        came = plan.swap(after(sums, evens), 0)
        here = conv_two(plan, 1, evens, range(frames // 2), kernel, F32)
        send = merge(plan, 0, here, came, range(1, frames, 2), BF16)
        here = conv_two(plan, 1, evens, range(frames // 2, frames), kernel, F32)
        return sum_rest(plan, here, came, send)
    cames = [plan.swap(part, 0) for part in conv_for_other(plan, odds, 1, kernel, 2)]
    own = conv_for_other(plan, odds, 0, kernel, 1)[0]
    near, both = after(evens[: plan.ratio], own), evens
    sums = conv_part(plan, 0, 0, near, kernel, cames, BF16)
    early = plan.swap(sums, 1)
    sums = conv_part(plan, 1, 0, after(both, sums), kernel, cames, BF16)
    late = plan.swap(sums, 1)
    early = after(early, sums)
    kept = conv_part(plan, 2, 1, after(both, early), kernel, [plan.swap(own, 0)], F32)
    body = functools.partial(put_body, plan)
    return plan.call(body, [kept, early, late], [(kept.shape, BF16)])[0]


def shards(mesh, features, kernel_one, kernel_two):
    plan = Plan(mesh, features, kernel_one)
    block = features.reshape(plan.pixels, plan.piece)
    odd = list(range(1, plan.cols, 2))
    even = list(range(2, plan.cols, 4)) + list(range(0, plan.cols, 4))
    early = [p for d in odd for p in plan.spread_frame(block, d)]
    kernel_one = stage(kernel_one)
    late = [p for d in even for p in plan.spread_frame(block, d)]
    last = plan.order[-1]
    keep, ahead = sum_one(plan, *conv_one_in_two(plan, early, kernel_one, 1))
    kept, cames = conv_one_in_two(plan, after(late, ahead), kernel_one, 2)
    kept, behind = sum_one(plan, kept, cames)
    hidden = join(plan, add_silu(plan, keep, after(plan.swap(ahead, last), behind)))
    odds = [p for t in range(plan.pairs) for p in plan.spread(hidden, 0, t)]
    hidden = join(plan, add_silu(plan, kept, plan.swap(behind, last)))
    evens = [p for t in range(plan.pairs) for p in plan.spread(hidden, 1, t)]
    return sum_in_parts(plan, odds, evens, hidden, kernel_two).reshape(features.shape)


def solution(mesh):
    placed = (
        P(("groups", "img"), None, None, "chan"),
        P(None, None, "img", "chan"),
        P(None, None, "img", "chan"),
    )
    return jax.shard_map(
        functools.partial(shards, mesh),
        mesh=mesh,
        in_specs=placed,
        out_specs=P(("groups", "img"), None, None, "chan"),
        check_vma=False,
    )
```
